512 devices in a mesh: seq: 64 (over x, z_hi, y), chan: 8 (over z_lo, core).
Axes of the slice: x: 4, y: 8, z: 8 (z_hi: 2, z_lo: 4; z = z_hi * 4 + z_lo), core: 2. Of those that a mesh axis runs over, the one named last changes fastest.
Arguments:
- values: bfloat16 [8192, 8192], P('seq', 'chan'), may hold values from -6 to 6
- gate: bfloat16 [8192, 8192], P('seq', 'chan'), may hold values from -6 to 6
- skip: float32 [8192], P('chan'), may hold values from 0.5 to 1.5
- spectrum: float32 [2, 128, 128, 8192], P(None, 'seq', None, 'chan'), may hold values from -8 to 8
- out_weight: bfloat16 [4096, 8192], P('seq', 'chan'), may hold values from -0.0625 to 0.0625
Outputs:
- result: bfloat16 [8192, 4096], P('seq', 'chan')
The draws below stay inside these ranges and needn't reach their ends.
All inputs are finite; a program needn't handle non-finite values.
Results may differ from the reference program's by a relative error of at most 0.0049.
Values may be sent and summed in bfloat16 or wider, within the bound.
A program may use at most 64 MiB of HBM per device.

```python
import jax
import jax.numpy as jnp
from jax import lax

D = 8192
DOUT = 4096
TOK_DEV = 128
L = 8192
NG = 128
M = 16384


def levels(stream_key, shape, split, least, high):
    level, own = 1.0, jax.random.fold_in(stream_key, 6)
    for axis_at, parts in split:
        heights = jnp.exp(jax.random.uniform(jax.random.fold_in(own, axis_at), (parts,), jnp.float32, least / len(split), high / len(split)))
        level = level * jnp.repeat(heights, shape[axis_at] // parts).reshape([-1 if axis == axis_at else 1 for axis in range(len(shape))])
    return level


def bell_draw(stream_key, extent, spread, bound, pieces=(), dtype=jnp.bfloat16):
    result = jax.random.normal(stream_key, extent, jnp.float32) * spread
    if len(pieces) > 0:
        result = levels(stream_key, extent, pieces, -0.22, 0.18) * result
    return jnp.clip(result, min=-bound, max=bound).astype(dtype)


def setup_inputs(seed: int = 0) -> dict:
    keys = jax.random.split(jax.random.key(seed), 6)
    return {
        "values": bell_draw(keys[0], (L, D), 1.0, 6.0, ((0, 64), (1, 8))),
        "gate": bell_draw(keys[1], (L, D), 1.0, 6.0, ((0, 64), (1, 8))),
        "skip": jnp.clip(0.5 + 1.0 * jax.random.uniform(keys[2], (D,), jnp.float32) ** levels(keys[2], (D,), ((0, 8),), -0.2, 0.2), 0.5, 1.5),
        "spectrum": bell_draw(keys[3], (2, NG, TOK_DEV, D), 1.4, 8.0, ((1, 64), (3, 8)), jnp.float32),
        "out_weight": bell_draw(keys[4], (DOUT, D), D ** -0.5, 0.0625, ((0, 64), (1, 8))),
    }


def reference(values, gate, skip, spectrum, out_weight):
    blocks = 8
    width = D // blocks
    padded = values.astype(jnp.float32)
    value_blocks = padded.reshape(L, blocks, width).transpose(1, 0, 2)
    spec_blocks = spectrum.reshape(2, NG, TOK_DEV, blocks, width).transpose(3, 0, 1, 2, 4)

    def convolve(pair):
        stream, spec = pair
        spec_v = jnp.fft.fft(stream, n=M, axis=0)
        kernel = (spec[0] + 1j * spec[1]).transpose(1, 0, 2).reshape(M, width)
        return jnp.fft.ifft(kernel * spec_v, axis=0)[:L].real

    conv = lax.map(convolve, (value_blocks, spec_blocks))
    conv = conv.transpose(1, 0, 2).reshape(L, D)
    mixed = (gate.astype(jnp.float32) * (conv + skip * padded)).astype(jnp.bfloat16)
    projected = jnp.dot(mixed, out_weight.T, preferred_element_type=jnp.float32)
    return projected.astype(jnp.bfloat16)
```

```python
import functools
import math

import jax
import jax.numpy as jnp
from jax import lax
from jax.experimental import pallas as pl
from jax.experimental.pallas import tpu as pltpu
from jax.sharding import PartitionSpec as P

high = lax.Precision.HIGHEST
MESH = pl.DeviceIdType.MESH


def wrap(a, n):
    return jnp.where(a >= n, a - n, a)


def each_partner(me, fn):
    x, z, y = me // 16, (me // 8) % 2, me % 8
    for dx in range(4):
        for dz in range(2):
            base = wrap(x + dx, 4) * 16 + (z if dz == 0 else 1 - z) * 8

            def step(dy, carry, base=base):
                fn(base + wrap(y + dy, 8))
                return carry

            lax.fori_loop(0 if dx or dz else 1, 8, step, 0)


def swap_kernel(n, x_ref, o_ref, send_sem, recv_sem, own_sem):
    me = lax.axis_index("seq")
    bar = pltpu.get_barrier_semaphore()
    each_partner(
        me,
        lambda t: pl.semaphore_signal(
            bar, inc=1, device_id={"seq": t}, device_id_type=MESH
        ),
    )
    own = pltpu.make_async_copy(x_ref.at[me], o_ref.at[me], own_sem)
    own.start()
    pl.semaphore_wait(bar, n - 1)

    def copy(src, dst, t):
        return pltpu.make_async_remote_copy(
            src_ref=src,
            dst_ref=dst,
            send_sem=send_sem,
            recv_sem=recv_sem,
            device_id={"seq": t},
            device_id_type=MESH,
        )

    each_partner(me, lambda t: copy(x_ref.at[t], o_ref.at[me], t).start())
    own.wait()
    rest = copy(x_ref.at[pl.ds(0, n - 1)], o_ref.at[pl.ds(0, n - 1)], me)
    rest.wait_send()
    rest.wait_recv()


def swap(x, cid):
    n = x.shape[0]
    flat = x.reshape(n, -1, 128)
    out = pl.pallas_call(
        functools.partial(swap_kernel, n),
        out_shape=jax.ShapeDtypeStruct(flat.shape, flat.dtype),
        in_specs=[pl.BlockSpec(memory_space=pltpu.VMEM)],
        out_specs=pl.BlockSpec(memory_space=pltpu.VMEM),
        scratch_shapes=[pltpu.SemaphoreType.DMA] * 3,
        compiler_params=pltpu.CompilerParams(
            collective_id=cid, has_side_effects=True, vmem_limit_bytes=32 * 2**20
        ),
    )(flat)
    return out.reshape(x.shape)


def angle_table(rows, cols, period):
    product = (
        jnp.arange(rows, dtype=jnp.int32)[:, None]
        * jnp.arange(cols, dtype=jnp.int32)[None, :]
        % period
    )
    theta = product.astype(jnp.float32) * (2.0 * math.pi / period)
    return (jnp.cos(theta), jnp.sin(theta))


def spectral_core(freq_re, freq_im, spec_re, spec_im, cos_hr, sin_hr):
    f_re = jnp.einsum("hr,grc->ghc", cos_hr, freq_re, precision=high) + jnp.einsum(
        "hr,grc->ghc", sin_hr, freq_im, precision=high
    )
    f_im = jnp.einsum("hr,grc->ghc", cos_hr, freq_im, precision=high) - jnp.einsum(
        "hr,grc->ghc", sin_hr, freq_re, precision=high
    )
    prod_re = f_re * spec_re - f_im * spec_im
    prod_im = f_re * spec_im + f_im * spec_re
    back_re = jnp.einsum("rh,ghc->grc", cos_hr, prod_re, precision=high) - jnp.einsum(
        "rh,ghc->grc", sin_hr, prod_im, precision=high
    )
    back_im = jnp.einsum("rh,ghc->grc", cos_hr, prod_im, precision=high) + jnp.einsum(
        "rh,ghc->grc", sin_hr, prod_re, precision=high
    )
    return (back_re, back_im)


def body(values, gate, skip, spectrum, out_weight):
    parts = lax.axis_size("seq")
    me_seq = lax.axis_index("seq")
    tok, chans = values.shape
    groups = 2 * parts
    total = groups * tok
    cos_ga, sin_ga = angle_table(groups, parts, groups)
    cos_hr, sin_hr = angle_table(tok, tok, tok)
    reach = tok // parts
    offsets = me_seq * reach + jnp.arange(reach, dtype=jnp.int32)
    twist = jnp.arange(groups, dtype=jnp.int32)[:, None] * offsets[None, :] % total
    twist = twist.astype(jnp.float32) * (2.0 * math.pi / total)
    cos_tw = jnp.cos(twist)[:, :, None]
    sin_tw = jnp.sin(twist)[:, :, None]
    moved = swap(values.reshape(parts, reach, chans), 0)
    gate_moved = swap(gate.reshape(parts, reach, chans), 1)
    stream = moved.astype(jnp.float32)
    part_re = jnp.einsum("ga,arc->grc", cos_ga, stream, precision=high)
    part_im = -jnp.einsum("ga,arc->grc", sin_ga, stream, precision=high)
    turned_re = part_re * cos_tw + part_im * sin_tw
    turned_im = part_im * cos_tw - part_re * sin_tw
    turned = jnp.stack([turned_re, turned_im], axis=1).astype(jnp.bfloat16)
    freq = swap(turned.reshape(parts, 2, 2, reach, chans), 2)
    freq = freq.transpose(2, 1, 0, 3, 4).reshape(2, 2, tok, chans).astype(jnp.float32)
    back_re, back_im = spectral_core(freq[0], freq[1], spectrum[0], spectrum[1], cos_hr, sin_hr)
    back = jnp.stack([back_re, back_im]).astype(jnp.bfloat16)
    back = back.reshape(2, 2, parts, reach, chans).transpose(2, 1, 0, 3, 4)
    spread = swap(back, 3).reshape(groups, 2, reach, chans).astype(jnp.float32)
    untwist_re = spread[:, 0] * cos_tw - spread[:, 1] * sin_tw
    untwist_im = spread[:, 1] * cos_tw + spread[:, 0] * sin_tw
    conv_part = (
        jnp.einsum("ga,grc->arc", cos_ga, untwist_re, precision=high)
        - jnp.einsum("ga,grc->arc", sin_ga, untwist_im, precision=high)
    ) * (1.0 / total)
    mixed = (gate_moved.astype(jnp.float32) * (conv_part + skip * stream)).astype(jnp.bfloat16)
    mixed = mixed.reshape(parts * reach, chans)
    partial_out = lax.dot_general(
        mixed,
        lax.all_gather(out_weight, "seq", axis=0, tiled=True),
        (((1,), (1,)), ((), ())),
        preferred_element_type=jnp.float32,
    )
    summed = lax.psum_scatter(partial_out, "chan", scatter_dimension=1, tiled=True)
    shaped = summed.reshape(parts, tok // parts, summed.shape[1])
    returned = swap(shaped, 4)
    return returned.reshape(tok, summed.shape[1]).astype(jnp.bfloat16)


def solution(mesh):
    placed = (
        P("seq", "chan"),
        P("seq", "chan"),
        P("chan"),
        P(None, "seq", None, "chan"),
        P("seq", "chan"),
    )
    return jax.shard_map(
        body, mesh=mesh, in_specs=placed, out_specs=P("seq", "chan"), check_vma=False
    )
```

```python
import functools
import math

import jax
import jax.numpy as jnp
import numpy as np
from jax import lax
from jax.experimental import pallas as pl
from jax.experimental.pallas import tpu as pltpu
from jax.sharding import PartitionSpec as P

MESH = pl.DeviceIdType.MESH
BF = jnp.bfloat16
F32 = jnp.float32
SEQ = 64
GRP = 72


def wrap(a, n):
    return jnp.where(a >= n, a - n, a)


def split(x):
    top = x.astype(BF)
    return top, (x - top.astype(F32)).astype(BF)


def tables():
    g = np.arange(GRP)
    live = (g <= 64).astype(np.float64)[:, None]
    a = np.arange(SEQ)
    turn = 2.0 * np.pi * ((g[:, None] * a[None, :]) % 128) / 128
    ahead = np.concatenate([np.cos(turn) * live, -np.sin(turn) * live])
    top = ahead.astype(BF)
    low = (ahead - top.astype(np.float64)).astype(BF)
    ahead = np.concatenate([top, low], axis=1)
    back = np.concatenate([np.cos(turn) * live, -np.sin(turn) * live]).T / 16384.0
    top = back.astype(BF)
    low = (back - top.astype(np.float64)).astype(BF)
    back = np.concatenate([top, top, low], axis=1)
    lane = np.arange(128)
    i_of = lane // 16
    r = 16 * i_of[None, None, :] + np.arange(16)[:, None, None]
    theta = 2.0 * np.pi * ((r * g[None, :, None]) % 16384) / 16384
    twist = np.stack([np.cos(theta), -np.sin(theta)], axis=1).astype(np.float32)
    same = (lane[:, None] % 16 == lane[None, :] % 16).astype(np.float64)
    turn = 2.0 * np.pi * ((i_of[:, None] * i_of[None, :]) % 8) / 8
    c, s = np.cos(turn) * same, np.sin(turn) * same
    lane_ahead = np.block([[c, -s], [s, c]])
    lane_back = np.block([[c, s], [-s, c]])
    lane_ahead = np.concatenate([lane_ahead, lane_ahead]).astype(BF)
    lane_back = np.concatenate([lane_back, lane_back]).astype(BF)
    turn = 2.0 * np.pi * (np.arange(16)[:, None] * i_of[None, :]) / 128
    small = np.stack([np.cos(turn), -np.sin(turn)]).astype(np.float32)
    return ahead, back, twist, lane_ahead, lane_back, small


def swap_lanes(x):
    x = list(x)
    block = lax.broadcasted_iota(jnp.int32, x[0].shape, 1) // 16
    for bit in (1, 2, 4):
        clear = (block // bit) % 2 == 0
        for p in range(8):
            if p & bit:
                continue
            q = p | bit
            u, v = x[p], x[q]
            x[p] = jnp.where(clear, u, pltpu.roll(v, 16 * bit, 1))
            x[q] = jnp.where(clear, pltpu.roll(u, 128 - 16 * bit, 1), v)
    return x


def fft(z, sign):
    n = len(z)
    if n == 1:
        return z
    even, odd = fft(z[0::2], sign), fft(z[1::2], sign)
    out = [None] * n
    for k in range(n // 2):
        re, im = odd[k]
        if k == 0:
            pass
        elif 4 * k == n:
            re, im = (-im, re) if sign > 0 else (im, -re)
        elif 8 * k == n or 8 * k == 3 * n:
            h = math.sqrt(0.5)
            c = h if 8 * k == n else -h
            if sign > 0:
                re, im = re * c - im * h, im * c + re * h
            else:
                re, im = re * c + im * h, im * c - re * h
        else:
            c = math.cos(2 * math.pi * k / n)
            s = sign * math.sin(2 * math.pi * k / n)
            re, im = re * c - im * s, re * s + im * c
        out[k] = (even[k][0] + re, even[k][1] + im)
        out[k + n // 2] = (even[k][0] - re, even[k][1] - im)
    return out


def conv_kernel(
    values_hbm, gate_hbm, skip_hbm, spec_hbm,
    ahead_hbm, back_hbm, twist_hbm, lane_ahead_hbm, lane_back_hbm, small_hbm,
    out_ref,
    values_ref, gate_ref, skip_ref, spec_ref,
    ahead_ref, back_ref, twist_ref, lane_ahead_ref, lane_back_ref, small_ref,
    send_v, recv_v, send_k, recv_k, send_c, recv_c,
    time_ref, low_ref, high_ref, first_ref, second_ref,
    in_sem, spec_sem, own_sem, send_sem, recv_sem,
):
    me = lax.axis_index("seq")
    x, z, y = me // 16, (me // 8) % 2, me % 8

    def other(dx, dz, dy):
        zt = z + dz - 2 * z * dz
        return wrap(x + dx, 4) * 16 + zt * 8 + wrap(y + dy, 8)

    def each_partner(fn):
        def step(i, carry):
            dx, dz, dy = i // 16, (i // 8) % 2, i % 8
            fn(other(dx, dz, dy))
            return carry

        lax.fori_loop(1, SEQ, step, 0)

    loads = []
    for at, (src, dst) in enumerate((
        (values_hbm, values_ref), (gate_hbm, gate_ref), (skip_hbm, skip_ref),
        (ahead_hbm, ahead_ref), (back_hbm, back_ref), (twist_hbm, twist_ref),
        (lane_ahead_hbm, lane_ahead_ref), (lane_back_hbm, lane_back_ref),
        (small_hbm, small_ref),
    )):
        load = pltpu.make_async_copy(src, dst, in_sem.at[at])
        load.start()
        loads.append(load)
    spec_loads = []
    for lt in range(8):
        load = pltpu.make_async_copy(
            spec_hbm.at[:, :, :, pl.ds(128 * lt, 128)], spec_ref.at[lt], spec_sem.at[lt]
        )
        load.start()
        spec_loads.append(load)

    bar = pltpu.get_barrier_semaphore()
    each_partner(
        lambda t: pl.semaphore_signal(
            bar, inc=1, device_id={"seq": t}, device_id_type=MESH
        )
    )

    def lanes(lt):
        return pl.ds(pl.multiple_of(128 * lt, 128), 128)

    def remote(src, dst, t, at):
        return pltpu.make_async_remote_copy(
            src_ref=src, dst_ref=dst, send_sem=send_sem.at[at], recv_sem=recv_sem.at[at],
            device_id={"seq": t}, device_id_type=MESH,
        )

    def all_sent(src, at):
        remote(src.at[pl.ds(0, SEQ - 1)], src.at[pl.ds(0, SEQ - 1)], me, at).wait_send()

    def all_here(dst, at):
        remote(dst.at[pl.ds(0, SEQ - 1)], dst.at[pl.ds(0, SEQ - 1)], me, at).wait_recv()

    loads[0].wait()

    def pack_values(lt, carry):
        tiles = swap_lanes(
            [values_ref[16 * i : 16 * i + 16, lanes(lt)].astype(F32) for i in range(8)]
        )
        for d in range(8):
            send_v[lt * 8 + d] = tiles[d].astype(BF)
        return carry

    lax.fori_loop(0, 8, pack_values, 0)
    own_v = pltpu.make_async_copy(send_v.at[me], recv_v.at[me], own_sem.at[0])
    own_v.start()
    pl.semaphore_wait(bar, SEQ - 1)
    each_partner(lambda t: remote(send_v.at[t], recv_v.at[me], t, 0).start())

    upper = me >= SEQ // 2
    slot = jnp.where(upper, 95 - me, me)
    for load in spec_loads:
        load.wait()

    def pack_spectrum(i, carry):
        dx, dz = i // 2, i % 2
        lt = wrap(x + dx, 4) * 2 + z + dz - 2 * z * dz

        def plane(q, inner):
            gl, part = q // 2, q % 2
            source = jnp.where(upper, 1 - gl, gl)
            tiles = swap_lanes([
                spec_ref[lt, part, source, pl.ds(jnp.where(upper, 7 - h, h), 16, stride=8), :]
                for h in range(8)
            ])
            for d in range(8):
                send_k[lt * 8 + d, pl.ds(pl.multiple_of(16 * q, 16), 16), :] = tiles[d].astype(BF)
            return inner

        lax.fori_loop(0, 4, plane, 0)

        @pl.when(i > 0)
        def _():
            t = lt * 8 + y
            remote(send_k.at[t], recv_k.at[slot], t, 1).start()

        def to_row(dy, inner):
            t = lt * 8 + wrap(y + dy, 8)
            remote(send_k.at[t], recv_k.at[slot], t, 1).start()
            return inner

        lax.fori_loop(1, 8, to_row, 0)
        return carry

    lax.fori_loop(0, 8, pack_spectrum, 0)
    own_k = pltpu.make_async_copy(send_k.at[me], recv_k.at[slot], own_sem.at[1])
    own_k.start()
    for load in loads[1:]:
        load.wait()

    own_v.wait()
    all_here(recv_v, 0)
    time_ref[...] = recv_v[...].reshape(SEQ * 16, 128).astype(F32)

    def over_a(jj, carry):
        pair = jnp.concatenate(
            [time_ref[pl.ds(2 * jj + b, SEQ, stride=16), :].astype(BF) for b in range(2)], axis=1
        )
        both = jnp.concatenate([pair, pair], axis=0)
        got = jnp.dot(ahead_ref[...], both, preferred_element_type=F32)
        for b in range(2):
            re, im = got[:GRP, 128 * b : 128 * b + 128], got[GRP:, 128 * b : 128 * b + 128]
            tr, ti = twist_ref[2 * jj + b, 0], twist_ref[2 * jj + b, 1]
            rows = pl.ds(pl.multiple_of((2 * jj + b) * GRP, 8), GRP)
            first_ref[rows, 0:128] = re * tr - im * ti
            first_ref[rows, 128:256] = re * ti + im * tr
        return carry

    lax.fori_loop(0, 8, over_a, 0)

    def over_lanes(src, table, dst):
        def step(b, carry):
            rows = pl.ds(pl.multiple_of(b * 288, 16), 288)
            top, low = split(src[rows, :])
            dst[rows, :] = jnp.dot(
                jnp.concatenate([top, low], axis=1), table[...], preferred_element_type=F32
            )
            return carry

        lax.fori_loop(0, 4, step, 0)

    over_lanes(first_ref, lane_ahead_ref, second_ref)

    own_k.wait()
    all_here(recv_k, 1)
    low_ref[pl.ds(64 * 32, 8 * 32), :] = jnp.zeros((8 * 32, 128), F32)
    high_ref[pl.ds(0, 32), :] = jnp.zeros((32, 128), F32)
    high_ref[pl.ds(65 * 32, 7 * 32), :] = jnp.zeros((7 * 32, 128), F32)

    def widen(b, carry):
        rows = pl.multiple_of(b * 256, 32)
        low_ref[pl.ds(rows, 256), :] = recv_k[pl.ds(4 * b, 4)].reshape(256, 128).astype(F32)
        high_ref[pl.ds(32 + rows, 256), :] = (
            recv_k[pl.ds(32 + 4 * b, 4)].reshape(256, 128).astype(F32)
        )
        return carry

    lax.fori_loop(0, 8, widen, 0)

    def filtered(b, carry):
        g = b * 8

        def rows(j):
            return pl.ds(pl.multiple_of(j * GRP + g, 8), 8)

        turned = []
        for j in range(16):
            re, im = second_ref[rows(j), 0:128], second_ref[rows(j), 128:256]
            if j:
                tr, ti = small_ref[0, j : j + 1, :], small_ref[1, j : j + 1, :]
                re, im = re * tr - im * ti, re * ti + im * tr
            turned.append((re, im))
        freq = fft(turned, -1)
        prod = []
        for h in range(16):
            re, im = freq[h]
            kr = (
                low_ref[pl.ds(g * 32 + h, 8, stride=32), :]
                + high_ref[pl.ds(g * 32 + 15 - h, 8, stride=32), :]
            )
            ki = (
                low_ref[pl.ds(g * 32 + 16 + h, 8, stride=32), :]
                - high_ref[pl.ds(g * 32 + 31 - h, 8, stride=32), :]
            )
            prod.append((re * kr - im * ki, re * ki + im * kr))
        spread = fft(prod, 1)
        for j in range(16):
            re, im = spread[j]
            if j:
                tr, ti = small_ref[0, j : j + 1, :], small_ref[1, j : j + 1, :]
                re, im = re * tr + im * ti, im * tr - re * ti
            first_ref[rows(j), 0:128] = re
            first_ref[rows(j), 128:256] = im
        return carry

    lax.fori_loop(0, GRP // 8, filtered, 0)
    over_lanes(first_ref, lane_back_ref, second_ref)

    def back_over_a(jj, carry):
        sides = []
        for b in range(2):
            rows = pl.ds(pl.multiple_of((2 * jj + b) * GRP, 8), GRP)
            re, im = second_ref[rows, 0:128], second_ref[rows, 128:256]
            tr, ti = twist_ref[2 * jj + b, 0], twist_ref[2 * jj + b, 1]
            sides.append(jnp.concatenate([re * tr + im * ti, im * tr - re * ti], axis=0))
        top, low = split(jnp.concatenate(sides, axis=1))
        got = jnp.dot(
            back_ref[...], jnp.concatenate([top, low, top], axis=0), preferred_element_type=F32
        )
        for b in range(2):
            time_ref[pl.ds(2 * jj + b, SEQ, stride=16), :] = got[:, 128 * b : 128 * b + 128]
        return carry

    lax.fori_loop(0, 8, back_over_a, 0)
    send_c[...] = time_ref[...].astype(BF).reshape(SEQ, 16, 128)
    own_c = pltpu.make_async_copy(send_c.at[me], recv_c.at[me], own_sem.at[2])
    own_c.start()
    each_partner(lambda t: remote(send_c.at[t], recv_c.at[me], t, 2).start())
    own_c.wait()
    all_here(recv_c, 2)

    def mix(lt, carry):
        tiles = swap_lanes([recv_c[lt * 8 + d].astype(F32) for d in range(8)])
        scale = skip_ref[0:1, lanes(lt)]
        for i in range(8):
            rows = slice(16 * i, 16 * i + 16)
            held = values_ref[rows, lanes(lt)].astype(F32)
            out_ref[rows, lanes(lt)] = (
                gate_ref[rows, lanes(lt)].astype(F32) * (tiles[i] + scale * held)
            ).astype(BF)
        return carry

    lax.fori_loop(0, 8, mix, 0)
    all_sent(send_v, 0)
    all_sent(send_k, 1)
    all_sent(send_c, 2)


def long_conv(values, gate, skip, spectrum):
    consts = [jnp.asarray(t) for t in tables()]
    arrays = [values, gate, skip.reshape(1, -1), spectrum] + consts
    vmem = lambda t: pltpu.VMEM(t.shape, t.dtype)
    held = [vmem(a) for a in arrays[:3]] + [pltpu.VMEM((8, 2, 2, 128, 128), F32)]
    held += [vmem(t) for t in consts]
    dma = pltpu.SemaphoreType.DMA
    return pl.pallas_call(
        conv_kernel,
        out_shape=jax.ShapeDtypeStruct(values.shape, BF),
        in_specs=[pl.BlockSpec(memory_space=pl.ANY)] * len(arrays),
        out_specs=pl.BlockSpec(memory_space=pltpu.VMEM),
        scratch_shapes=held
        + [pltpu.VMEM((SEQ, 16, 128), BF)] * 2
        + [pltpu.VMEM((SEQ, 64, 128), BF)] * 2
        + [pltpu.VMEM((SEQ, 16, 128), BF)] * 2
        + [pltpu.VMEM((SEQ * 16, 128), F32)]
        + [pltpu.VMEM((GRP * 32, 128), F32)] * 2
        + [pltpu.VMEM((GRP * 16, 256), F32)] * 2
        + [dma((9,)), dma((8,)), dma((3,)), dma((3,)), dma((3,))],
        compiler_params=pltpu.CompilerParams(
            collective_id=0, has_side_effects=True, vmem_limit_bytes=40 * 2**20
        ),
        name="long_conv",
    )(*arrays)


def body(values, gate, skip, spectrum, out_weight):
    mixed = long_conv(values, gate, skip, spectrum)
    partial_out = lax.dot_general(
        mixed,
        lax.all_gather(out_weight, "seq", axis=0, tiled=True),
        (((1,), (1,)), ((), ())),
        preferred_element_type=F32,
    )
    return lax.psum_scatter(partial_out, "chan", scatter_dimension=1, tiled=True).astype(BF)


def solution(mesh):
    placed = (
        P("seq", "chan"),
        P("seq", "chan"),
        P("chan"),
        P(None, "seq", None, "chan"),
        P("seq", "chan"),
    )
    return jax.shard_map(
        body, mesh=mesh, in_specs=placed, out_specs=P("seq", "chan"), check_vma=False
    )
```

```python
import functools
import math

import jax
import jax.numpy as jnp
import numpy as np
from jax import lax
from jax.experimental import pallas as pl
from jax.experimental.pallas import tpu as pltpu
from jax.sharding import PartitionSpec as P

MESH = pl.DeviceIdType.MESH
BF = jnp.bfloat16
F32 = jnp.float32
SEQ = 64
GRP = 72


def wrap(a, n):
    return jnp.where(a >= n, a - n, a)


def split(x):
    top = x.astype(BF)
    return top, (x - top.astype(F32)).astype(BF)


def tables():
    g = np.arange(GRP)
    live = (g <= 64).astype(np.float64)[:, None]
    a = np.arange(SEQ)
    turn = 2.0 * np.pi * ((g[:, None] * a[None, :]) % 128) / 128
    ahead = np.concatenate([np.cos(turn) * live, -np.sin(turn) * live])
    top = ahead.astype(BF)
    low = (ahead - top.astype(np.float64)).astype(BF)
    ahead = np.concatenate([top, low], axis=1)
    back = np.concatenate([np.cos(turn) * live, -np.sin(turn) * live]).T / 16384.0
    top = back.astype(BF)
    low = (back - top.astype(np.float64)).astype(BF)
    back = np.concatenate([top, top, low], axis=1)
    lane = np.arange(128)
    i_of = lane // 16
    r = 16 * i_of[None, None, :] + np.arange(16)[:, None, None]
    theta = 2.0 * np.pi * ((r * g[None, :, None]) % 16384) / 16384
    twist = np.stack([np.cos(theta), -np.sin(theta)], axis=1).astype(np.float32)
    same = (lane[:, None] % 16 == lane[None, :] % 16).astype(np.float64)
    turn = 2.0 * np.pi * ((i_of[:, None] * i_of[None, :]) % 8) / 8
    c, s = np.cos(turn) * same, np.sin(turn) * same
    lane_ahead = np.block([[c, -s], [s, c]])
    lane_back = np.block([[c, s], [-s, c]])
    lane_ahead = np.concatenate([lane_ahead, lane_ahead]).astype(BF)
    lane_back = np.concatenate([lane_back, lane_back]).astype(BF)
    turn = 2.0 * np.pi * (np.arange(16)[:, None] * i_of[None, :]) / 128
    small = np.stack([np.cos(turn), -np.sin(turn)]).astype(np.float32)
    return ahead, back, twist, lane_ahead, lane_back, small


def swap_lanes(x):
    x = list(x)
    block = lax.broadcasted_iota(jnp.int32, x[0].shape, 1) // 16
    for bit in (1, 2, 4):
        clear = (block // bit) % 2 == 0
        for p in range(8):
            if p & bit:
                continue
            q = p | bit
            u, v = x[p], x[q]
            x[p] = jnp.where(clear, u, pltpu.roll(v, 16 * bit, 1))
            x[q] = jnp.where(clear, pltpu.roll(u, 128 - 16 * bit, 1), v)
    return x


def fft(z, sign):
    n = len(z)
    if n == 1:
        return z
    even, odd = fft(z[0::2], sign), fft(z[1::2], sign)
    out = [None] * n
    for k in range(n // 2):
        re, im = odd[k]
        if k == 0:
            pass
        elif 4 * k == n:
            re, im = (-im, re) if sign > 0 else (im, -re)
        elif 8 * k == n or 8 * k == 3 * n:
            h = math.sqrt(0.5)
            c = h if 8 * k == n else -h
            if sign > 0:
                re, im = re * c - im * h, im * c + re * h
            else:
                re, im = re * c + im * h, im * c - re * h
        else:
            c = math.cos(2 * math.pi * k / n)
            s = sign * math.sin(2 * math.pi * k / n)
            re, im = re * c - im * s, re * s + im * c
        out[k] = (even[k][0] + re, even[k][1] + im)
        out[k + n // 2] = (even[k][0] - re, even[k][1] - im)
    return out


def block_kernel(
    values_hbm, gate_hbm, skip_hbm, spec_hbm, weight_hbm,
    ahead_hbm, back_hbm, twist_hbm, lane_ahead_hbm, lane_back_hbm, small_hbm,
    out_ref,
    values_ref, gate_ref, skip_ref, spec_ref,
    ahead_ref, back_ref, twist_ref, lane_ahead_ref, lane_back_ref, small_ref,
    send_v, recv_v, send_k, recv_k, send_c, recv_c,
    time_ref, low_ref, high_ref, first_ref, second_ref,
    w_ref, mixed_ref, recv_m, half_send, half_recv, own_half, z_send, z_recv, done,
    in_sem, spec_sem, own_sem, send_sem, recv_sem,
    ring_send, ring_recv, m_send, m_recv, h_send, h_recv, zs_sem, zr_sem, o_sem,
):
    me, ch = lax.axis_index("seq"), lax.axis_index("chan")
    x, z, y = me // 16, (me // 8) % 2, me % 8
    low = me % 16
    zl, core = ch // 2, ch % 2
    cross = x != zl

    def other(dx, dz, dy):
        zt = z + dz - 2 * z * dz
        return wrap(x + dx, 4) * 16 + zt * 8 + wrap(y + dy, 8)

    def each_partner(fn):
        def step(i, carry):
            dx, dz, dy = i // 16, (i // 8) % 2, i % 8
            fn(other(dx, dz, dy))
            return carry

        lax.fori_loop(1, SEQ, step, 0)

    loads = []
    for at, (src, dst) in enumerate((
        (values_hbm, values_ref), (gate_hbm, gate_ref), (skip_hbm, skip_ref),
        (ahead_hbm, ahead_ref), (back_hbm, back_ref), (twist_hbm, twist_ref),
        (lane_ahead_hbm, lane_ahead_ref), (lane_back_hbm, lane_back_ref),
        (small_hbm, small_ref),
    )):
        load = pltpu.make_async_copy(src, dst, in_sem.at[at])
        load.start()
        loads.append(load)
    spec_loads = []
    for lt in range(8):
        load = pltpu.make_async_copy(
            spec_hbm.at[:, :, :, pl.ds(128 * lt, 128)], spec_ref.at[lt], spec_sem.at[lt]
        )
        load.start()
        spec_loads.append(load)

    bar = pltpu.get_barrier_semaphore()

    def greet(seq, chan):
        pl.semaphore_signal(
            bar, inc=1, device_id={"seq": seq, "chan": chan}, device_id_type=MESH
        )

    each_partner(lambda t: greet(t, ch))
    for d in (1, 2, 3):
        greet(me, wrap(zl + d, 4) * 2 + core)
    greet(me, zl * 2 + 1 - core)

    @pl.when(cross)
    def _():
        greet(zl * 16 + low, x * 2 + core)

    def link(src, dst, ss, rs, seq, chan):
        return pltpu.make_async_remote_copy(
            src_ref=src, dst_ref=dst, send_sem=ss, recv_sem=rs,
            device_id={"seq": seq, "chan": chan}, device_id_type=MESH,
        )

    def lanes(lt):
        return pl.ds(pl.multiple_of(128 * lt, 128), 128)

    def remote(src, dst, t, at):
        return pltpu.make_async_remote_copy(
            src_ref=src, dst_ref=dst, send_sem=send_sem.at[at], recv_sem=recv_sem.at[at],
            device_id={"seq": t}, device_id_type=MESH,
        )

    def all_sent(src, at):
        remote(src.at[pl.ds(0, SEQ - 1)], src.at[pl.ds(0, SEQ - 1)], me, at).wait_send()

    def all_here(dst, at):
        remote(dst.at[pl.ds(0, SEQ - 1)], dst.at[pl.ds(0, SEQ - 1)], me, at).wait_recv()

    loads[0].wait()

    def pack_values(lt, carry):
        tiles = swap_lanes(
            [values_ref[16 * i : 16 * i + 16, lanes(lt)].astype(F32) for i in range(8)]
        )
        for d in range(8):
            send_v[lt * 8 + d] = tiles[d].astype(BF)
        return carry

    lax.fori_loop(0, 8, pack_values, 0)
    own_v = pltpu.make_async_copy(send_v.at[me], recv_v.at[me], own_sem.at[0])
    own_v.start()
    pl.semaphore_wait(bar, jnp.where(cross, SEQ + 4, SEQ + 3))
    own_w = pltpu.make_async_copy(weight_hbm, w_ref.at[z, y], own_sem.at[3])
    own_w.start()
    pair_w = link(
        weight_hbm, w_ref.at[z, y], ring_send.at[0, 0], ring_recv.at[0, 0],
        x * 16 + (1 - z) * 8 + y, ch,
    )
    pair_w.start()
    each_partner(lambda t: remote(send_v.at[t], recv_v.at[me], t, 0).start())

    upper = me >= SEQ // 2
    slot = jnp.where(upper, 95 - me, me)
    for load in spec_loads:
        load.wait()

    def pack_spectrum(i, carry):
        dx, dz = i // 2, i % 2
        lt = wrap(x + dx, 4) * 2 + z + dz - 2 * z * dz

        def plane(q, inner):
            gl, part = q // 2, q % 2
            source = jnp.where(upper, 1 - gl, gl)
            tiles = swap_lanes([
                spec_ref[lt, part, source, pl.ds(jnp.where(upper, 7 - h, h), 16, stride=8), :]
                for h in range(8)
            ])
            for d in range(8):
                send_k[lt * 8 + d, pl.ds(pl.multiple_of(16 * q, 16), 16), :] = tiles[d].astype(BF)
            return inner

        lax.fori_loop(0, 4, plane, 0)

        @pl.when(i > 0)
        def _():
            t = lt * 8 + y
            remote(send_k.at[t], recv_k.at[slot], t, 1).start()

        def to_row(dy, inner):
            t = lt * 8 + wrap(y + dy, 8)
            remote(send_k.at[t], recv_k.at[slot], t, 1).start()
            return inner

        lax.fori_loop(1, 8, to_row, 0)
        return carry

    lax.fori_loop(0, 8, pack_spectrum, 0)
    own_k = pltpu.make_async_copy(send_k.at[me], recv_k.at[slot], own_sem.at[1])
    own_k.start()
    for load in loads[1:]:
        load.wait()

    def ring(step, way):
        at = wrap(y + (9 - step if way == 0 else step - 1), 8)
        block = w_ref.at[:, at] if step < 4 else w_ref.at[way, at]
        to = wrap(y + (1 if way == 0 else 7), 8)
        return link(
            block, block, ring_send.at[way, step], ring_recv.at[way, step], x * 16 + z * 8 + to, ch
        )

    def ring_step(step):
        for way in range(2):
            if step > 1:
                ring(step - 1, way).wait_recv()
            ring(step, way).start()

    own_v.wait()
    all_here(recv_v, 0)
    own_w.wait()
    pair_w.wait_recv()
    ring_step(1)
    time_ref[...] = recv_v[...].reshape(SEQ * 16, 128).astype(F32)

    def over_a(jj, carry):
        pair = jnp.concatenate(
            [time_ref[pl.ds(2 * jj + b, SEQ, stride=16), :].astype(BF) for b in range(2)], axis=1
        )
        both = jnp.concatenate([pair, pair], axis=0)
        got = jnp.dot(ahead_ref[...], both, preferred_element_type=F32)
        for b in range(2):
            re, im = got[:GRP, 128 * b : 128 * b + 128], got[GRP:, 128 * b : 128 * b + 128]
            tr, ti = twist_ref[2 * jj + b, 0], twist_ref[2 * jj + b, 1]
            rows = pl.ds(pl.multiple_of((2 * jj + b) * GRP, 8), GRP)
            first_ref[rows, 0:128] = re * tr - im * ti
            first_ref[rows, 128:256] = re * ti + im * tr
        return carry

    lax.fori_loop(0, 8, over_a, 0)

    def over_lanes(src, table, dst):
        def step(b, carry):
            rows = pl.ds(pl.multiple_of(b * 288, 16), 288)
            top, low = split(src[rows, :])
            dst[rows, :] = jnp.dot(
                jnp.concatenate([top, low], axis=1), table[...], preferred_element_type=F32
            )
            return carry

        lax.fori_loop(0, 4, step, 0)

    over_lanes(first_ref, lane_ahead_ref, second_ref)

    own_k.wait()
    all_here(recv_k, 1)
    ring_step(2)
    low_ref[pl.ds(64 * 32, 8 * 32), :] = jnp.zeros((8 * 32, 128), F32)
    high_ref[pl.ds(0, 32), :] = jnp.zeros((32, 128), F32)
    high_ref[pl.ds(65 * 32, 7 * 32), :] = jnp.zeros((7 * 32, 128), F32)

    def widen(b, carry):
        rows = pl.multiple_of(b * 256, 32)
        low_ref[pl.ds(rows, 256), :] = recv_k[pl.ds(4 * b, 4)].reshape(256, 128).astype(F32)
        high_ref[pl.ds(32 + rows, 256), :] = (
            recv_k[pl.ds(32 + 4 * b, 4)].reshape(256, 128).astype(F32)
        )
        return carry

    lax.fori_loop(0, 8, widen, 0)

    def filtered(b, carry):
        g = b * 8

        def rows(j):
            return pl.ds(pl.multiple_of(j * GRP + g, 8), 8)

        turned = []
        for j in range(16):
            re, im = second_ref[rows(j), 0:128], second_ref[rows(j), 128:256]
            if j:
                tr, ti = small_ref[0, j : j + 1, :], small_ref[1, j : j + 1, :]
                re, im = re * tr - im * ti, re * ti + im * tr
            turned.append((re, im))
        freq = fft(turned, -1)
        prod = []
        for h in range(16):
            re, im = freq[h]
            kr = (
                low_ref[pl.ds(g * 32 + h, 8, stride=32), :]
                + high_ref[pl.ds(g * 32 + 15 - h, 8, stride=32), :]
            )
            ki = (
                low_ref[pl.ds(g * 32 + 16 + h, 8, stride=32), :]
                - high_ref[pl.ds(g * 32 + 31 - h, 8, stride=32), :]
            )
            prod.append((re * kr - im * ki, re * ki + im * kr))
        spread = fft(prod, 1)
        for j in range(16):
            re, im = spread[j]
            if j:
                tr, ti = small_ref[0, j : j + 1, :], small_ref[1, j : j + 1, :]
                re, im = re * tr + im * ti, im * tr - re * ti
            first_ref[rows(j), 0:128] = re
            first_ref[rows(j), 128:256] = im
        return carry

    lax.fori_loop(0, GRP // 8, filtered, 0)
    over_lanes(first_ref, lane_back_ref, second_ref)

    def back_over_a(jj, carry):
        sides = []
        for b in range(2):
            rows = pl.ds(pl.multiple_of((2 * jj + b) * GRP, 8), GRP)
            re, im = second_ref[rows, 0:128], second_ref[rows, 128:256]
            tr, ti = twist_ref[2 * jj + b, 0], twist_ref[2 * jj + b, 1]
            sides.append(jnp.concatenate([re * tr + im * ti, im * tr - re * ti], axis=0))
        top, low = split(jnp.concatenate(sides, axis=1))
        got = jnp.dot(
            back_ref[...], jnp.concatenate([top, low, top], axis=0), preferred_element_type=F32
        )
        for b in range(2):
            time_ref[pl.ds(2 * jj + b, SEQ, stride=16), :] = got[:, 128 * b : 128 * b + 128]
        return carry

    lax.fori_loop(0, 8, back_over_a, 0)
    send_c[...] = time_ref[...].astype(BF).reshape(SEQ, 16, 128)
    own_c = pltpu.make_async_copy(send_c.at[me], recv_c.at[me], own_sem.at[2])
    own_c.start()
    each_partner(lambda t: remote(send_c.at[t], recv_c.at[me], t, 2).start())
    ring_step(3)
    own_c.wait()
    all_here(recv_c, 2)
    ring_step(4)

    def mix(lt, carry):
        tiles = swap_lanes([recv_c[lt * 8 + d].astype(F32) for d in range(8)])
        scale = skip_ref[0:1, lanes(lt)]
        for i in range(8):
            rows = slice(16 * i, 16 * i + 16)
            held = values_ref[rows, lanes(lt)].astype(F32)
            mixed_ref[rows, lanes(lt)] = (
                gate_ref[rows, lanes(lt)].astype(F32) * (tiles[i] + scale * held)
            ).astype(BF)
        return carry

    lax.fori_loop(0, 8, mix, 0)
    for d in (1, 3, 2):
        link(
            mixed_ref, recv_m.at[d], m_send.at[d], m_recv.at[d], wrap(x + d, 4) * 16 + low, ch
        ).start()
    for way in range(2):
        ring(4, way).wait_recv()
    order = (0, 1, 3, 2)

    def half_copy(d):
        return link(
            half_send.at[d], half_recv.at[d], h_send.at[d], h_recv.at[d], me, zl * 2 + 1 - core
        )

    def multiply(d):
        src = mixed_ref
        if d:
            link(mixed_ref, recv_m.at[d], m_send.at[d], m_recv.at[d], me, ch).wait_recv()
            src = recv_m.at[d]
        for side in range(2):
            half = 1 - core if side == 0 else core
            got = lax.dot_general(
                src[...], w_ref[half].reshape(512, 1024), (((1,), (1,)), ((), ())),
                preferred_element_type=F32,
            )
            if side == 0:
                half_send[d] = got.astype(BF)
                half_copy(d).start()
            else:
                own_half[d] = got

    def pass_on(d):
        half_copy(d).wait_recv()
        target = wrap(x + 4 - d, 4)
        total = own_half[d] + half_recv[d].astype(F32)

        @pl.when(target == zl)
        def _():
            done[...] = total

        @pl.when(target != zl)
        def _():
            z_send[d] = total.astype(BF)
            link(
                z_send.at[d], z_recv.at[zl], zs_sem.at[d], zr_sem.at[zl], me, target * 2 + core
            ).start()

    for at, d in enumerate(order):
        multiply(d)
        if at:
            pass_on(order[at - 1])
    pass_on(order[-1])
    for d in (1, 2, 3):
        peer = wrap(zl + d, 4)
        link(z_send.at[0], z_recv.at[peer], zs_sem.at[0], zr_sem.at[peer], me, ch).wait_recv()
        done[...] += z_recv[peer].astype(F32)

    @pl.when(cross)
    def _():
        z_send[4] = done[...].astype(BF)
        last = link(z_send.at[4], out_ref, o_sem.at[0], o_sem.at[1], zl * 16 + low, x * 2 + core)
        last.start()
        last.wait()

    @pl.when(jnp.logical_not(cross))
    def _():
        out_ref[...] = done[...].astype(BF)

    for d in range(4):
        half_copy(d).wait_send()

        @pl.when(wrap(x + 4 - d, 4) != zl)
        def _(d=d):
            link(z_send.at[d], z_recv.at[0], zs_sem.at[d], zr_sem.at[0], me, ch).wait_send()

        if d:
            link(mixed_ref, recv_m.at[d], m_send.at[d], m_recv.at[d], me, ch).wait_send()
    all_sent(send_v, 0)
    all_sent(send_k, 1)
    all_sent(send_c, 2)
    pair_w.wait_send()
    for step in (1, 2, 3, 4):
        for way in range(2):
            ring(step, way).wait_send()


def block(values, gate, skip, spectrum, weight):
    consts = [jnp.asarray(t) for t in tables()]
    arrays = [values, gate, skip.reshape(1, -1), spectrum, weight] + consts
    vmem = lambda t: pltpu.VMEM(t.shape, t.dtype)
    held = [vmem(a) for a in arrays[:3]] + [pltpu.VMEM((8, 2, 2, 128, 128), F32)]
    held += [vmem(t) for t in consts]
    dma = pltpu.SemaphoreType.DMA
    return pl.pallas_call(
        block_kernel,
        out_shape=jax.ShapeDtypeStruct((128, 512), BF),
        in_specs=[pl.BlockSpec(memory_space=pltpu.HBM)] * len(arrays),
        out_specs=pl.BlockSpec(memory_space=pltpu.VMEM),
        scratch_shapes=held
        + [pltpu.VMEM((SEQ, 16, 128), BF)] * 2
        + [pltpu.VMEM((SEQ, 64, 128), BF)] * 2
        + [pltpu.VMEM((SEQ, 16, 128), BF)] * 2
        + [pltpu.VMEM((SEQ * 16, 128), F32)]
        + [pltpu.VMEM((GRP * 32, 128), F32)] * 2
        + [pltpu.VMEM((GRP * 16, 256), F32)] * 2
        + [
            pltpu.VMEM((2, 8, 64, 1024), BF),
            pltpu.VMEM((128, 1024), BF),
            pltpu.VMEM((4, 128, 1024), BF),
            pltpu.VMEM((4, 128, 512), BF),
            pltpu.VMEM((4, 128, 512), BF),
            pltpu.VMEM((4, 128, 512), F32),
            pltpu.VMEM((5, 128, 512), BF),
            pltpu.VMEM((4, 128, 512), BF),
            pltpu.VMEM((128, 512), F32),
        ]
        + [dma((9,)), dma((8,)), dma((4,)), dma((3,)), dma((3,))]
        + [dma((2, 5))] * 2
        + [dma((4,))] * 6
        + [dma((2,))],
        compiler_params=pltpu.CompilerParams(
            collective_id=0, has_side_effects=True, vmem_limit_bytes=63 * 2**20
        ),
        name="hyena_block",
    )(*arrays)


def solution(mesh):
    placed = (
        P("seq", "chan"),
        P("seq", "chan"),
        P("chan"),
        P(None, "seq", None, "chan"),
        P("seq", "chan"),
    )
    return jax.shard_map(
        block, mesh=mesh, in_specs=placed, out_specs=P("seq", "chan"), check_vma=False
    )
```

```python
import functools
import math

import jax
import jax.numpy as jnp
import numpy as np
from jax import lax
from jax.experimental import pallas as pl
from jax.experimental.pallas import tpu as pltpu
from jax.sharding import PartitionSpec as P

MESH = pl.DeviceIdType.MESH
BF = jnp.bfloat16
F32 = jnp.float32
SEQ = 64
GRP = 72


def wrap(a, n):
    return jnp.where(a >= n, a - n, a)


def split(x):
    top = x.astype(BF)
    return top, (x - top.astype(F32)).astype(BF)


def tables():
    g = np.arange(GRP)
    live = (g <= 64).astype(np.float64)[:, None]
    a = np.arange(SEQ)
    turn = 2.0 * np.pi * ((g[:, None] * a[None, :]) % 128) / 128
    ahead = np.concatenate([np.cos(turn) * live, -np.sin(turn) * live])
    top = ahead.astype(BF)
    low = (ahead - top.astype(np.float64)).astype(BF)
    ahead = np.concatenate([top, low], axis=1)
    back = np.concatenate([np.cos(turn) * live, -np.sin(turn) * live]).T / 16384.0
    top = back.astype(BF)
    low = (back - top.astype(np.float64)).astype(BF)
    back = np.concatenate([top, top, low], axis=1)
    lane = np.arange(128)
    i_of = lane // 16
    r = 16 * i_of[None, None, :] + np.arange(16)[:, None, None]
    theta = 2.0 * np.pi * ((r * g[None, :, None]) % 16384) / 16384
    twist = np.stack([np.cos(theta), -np.sin(theta)], axis=1).astype(np.float32)
    same = (lane[:, None] % 16 == lane[None, :] % 16).astype(np.float64)
    turn = 2.0 * np.pi * ((i_of[:, None] * i_of[None, :]) % 8) / 8
    c, s = np.cos(turn) * same, np.sin(turn) * same
    lane_ahead = np.block([[c, -s], [s, c]])
    lane_back = np.block([[c, s], [-s, c]])
    lane_ahead = np.concatenate([lane_ahead, lane_ahead]).astype(BF)
    lane_back = np.concatenate([lane_back, lane_back]).astype(BF)
    turn = 2.0 * np.pi * (np.arange(16)[:, None] * i_of[None, :]) / 128
    small = np.stack([np.cos(turn), -np.sin(turn)]).astype(np.float32)
    return ahead, back, twist, lane_ahead, lane_back, small


def swap_lanes(x):
    x = list(x)
    block = lax.broadcasted_iota(jnp.int32, x[0].shape, 1) // 16
    for bit in (1, 2, 4):
        clear = (block // bit) % 2 == 0
        for p in range(8):
            if p & bit:
                continue
            q = p | bit
            u, v = x[p], x[q]
            x[p] = jnp.where(clear, u, pltpu.roll(v, 16 * bit, 1))
            x[q] = jnp.where(clear, pltpu.roll(u, 128 - 16 * bit, 1), v)
    return x


def fft(z, sign):
    n = len(z)
    if n == 1:
        return z
    even, odd = fft(z[0::2], sign), fft(z[1::2], sign)
    out = [None] * n
    for k in range(n // 2):
        re, im = odd[k]
        if k == 0:
            pass
        elif 4 * k == n:
            re, im = (-im, re) if sign > 0 else (im, -re)
        elif 8 * k == n or 8 * k == 3 * n:
            h = math.sqrt(0.5)
            c = h if 8 * k == n else -h
            if sign > 0:
                re, im = re * c - im * h, im * c + re * h
            else:
                re, im = re * c + im * h, im * c - re * h
        else:
            c = math.cos(2 * math.pi * k / n)
            s = sign * math.sin(2 * math.pi * k / n)
            re, im = re * c - im * s, re * s + im * c
        out[k] = (even[k][0] + re, even[k][1] + im)
        out[k + n // 2] = (even[k][0] - re, even[k][1] - im)
    return out


def block_kernel(
    values_hbm, gate_hbm, skip_hbm, spec_hbm, weight_hbm,
    ahead_hbm, back_hbm, twist_hbm, lane_ahead_hbm, lane_back_hbm, small_hbm,
    out_ref,
    values_ref, gate_ref, skip_ref, spec_ref,
    ahead_ref, back_ref, twist_ref, lane_ahead_ref, lane_back_ref, small_ref,
    send_v, recv_v, send_k, recv_k, send_c, recv_c,
    time_ref, filter_ref, first_ref, second_ref,
    w_ref, mixed_ref, recv_m, half_send, half_recv, own_half, z_send, z_recv, done, ordered, final,
    in_sem, spec_sem, own_sem, send_sem, recv_sem,
    ring_send, ring_recv, m_send, m_recv, h_send, h_recv, zs_sem, zr_sem, o_sem, c_recv, k_recv,
):
    me, ch = lax.axis_index("seq"), lax.axis_index("chan")
    x, z, y = me // 16, (me // 8) % 2, me % 8
    low = me % 16
    zl, core = ch // 2, ch % 2
    cross = x != zl

    xs = [wrap(x + d, 4) * 16 for d in range(4)]
    zs = [z * 8, 8 - z * 8]
    ys = [wrap(y + d, 8) for d in range(8)]
    partners = [
        xs[dx] + zs[dz] + ys[dy]
        for dx in range(4) for half in range(2) for dy in range(8)
        for dz in ((half + dy) % 2,) if dx or dz or dy
    ]

    def each_partner(fn):
        for t in partners:
            fn(t)

    loads = []
    for at, (src, dst) in enumerate((
        (values_hbm, values_ref), (gate_hbm, gate_ref), (skip_hbm, skip_ref),
        (ahead_hbm, ahead_ref), (back_hbm, back_ref), (twist_hbm, twist_ref),
        (lane_ahead_hbm, lane_ahead_ref), (lane_back_hbm, lane_back_ref),
        (small_hbm, small_ref),
    )):
        load = pltpu.make_async_copy(src, dst, in_sem.at[at])
        load.start()
        loads.append(load)
    spec_loads = []
    for lt in range(8):
        load = pltpu.make_async_copy(
            spec_hbm.at[:, :, :, pl.ds(128 * lt, 128)], spec_ref.at[lt], spec_sem.at[lt]
        )
        load.start()
        spec_loads.append(load)

    bar = pltpu.get_barrier_semaphore()

    def greet(seq, chan):
        pl.semaphore_signal(
            bar, inc=1, device_id={"seq": seq, "chan": chan}, device_id_type=MESH
        )

    each_partner(lambda t: greet(t, ch))
    for d in (1, 2, 3):
        greet(me, wrap(zl + d, 4) * 2 + core)
    greet(me, zl * 2 + 1 - core)

    @pl.when(cross)
    def _():
        greet(zl * 16 + low, x * 2 + core)

    def link(src, dst, ss, rs, seq, chan):
        return pltpu.make_async_remote_copy(
            src_ref=src, dst_ref=dst, send_sem=ss, recv_sem=rs,
            device_id={"seq": seq, "chan": chan}, device_id_type=MESH,
        )

    def lanes(lt):
        return pl.ds(pl.multiple_of(128 * lt, 128), 128)

    def remote(src, dst, t, at, here=None):
        return pltpu.make_async_remote_copy(
            src_ref=src, dst_ref=dst, send_sem=send_sem.at[at],
            recv_sem=recv_sem.at[at] if here is None else here,
            device_id={"seq": t}, device_id_type=MESH,
        )

    def all_sent(src, at):
        remote(src.at[pl.ds(0, SEQ - 1)], src.at[pl.ds(0, SEQ - 1)], me, at).wait_send()

    def all_here(dst, at):
        remote(dst.at[pl.ds(0, SEQ - 1)], dst.at[pl.ds(0, SEQ - 1)], me, at).wait_recv()

    loads[0].wait()

    def pack_values(pair, carry):
        for lt in (2 * pair, 2 * pair + 1):
            tiles = swap_lanes(
                [values_ref[16 * i : 16 * i + 16, lanes(lt)].astype(F32) for i in range(8)]
            )
            for d in range(8):
                send_v[lt * 8 + d] = tiles[d].astype(BF)
        return carry

    lax.fori_loop(0, 4, pack_values, 0)
    own_v = pltpu.make_async_copy(send_v.at[me], recv_v.at[me], own_sem.at[0])
    own_v.start()
    pl.semaphore_wait(bar, jnp.where(cross, SEQ + 4, SEQ + 3))
    own_w = pltpu.make_async_copy(weight_hbm, w_ref.at[z, 0], own_sem.at[3])
    own_w.start()
    pair_w = link(
        weight_hbm, w_ref.at[z, 0], ring_send.at[0, 0], ring_recv.at[0, 0],
        x * 16 + (1 - z) * 8 + y, ch,
    )
    pair_w.start()
    each_partner(lambda t: remote(send_v.at[t], recv_v.at[me], t, 0).start())

    upper = me >= SEQ // 2
    slot = jnp.where(upper, 95 - me, me)
    for load in spec_loads:
        load.wait()

    def pack_spectrum(dx, carry):
        column = wrap(x + dx, 4) * 16
        for dz in range(2):
            lt = wrap(x + dx, 4) * 2 + z + dz - 2 * z * dz
            for q in range(4):
                gl, part = q // 2, q % 2
                source = jnp.where(upper, 1 - gl, gl)
                tiles = swap_lanes([
                    spec_ref[lt, part, source, pl.ds(jnp.where(upper, 7 - h, h), 16, stride=8), :]
                    for h in range(8)
                ])
                for d in range(8):
                    send_k[lt * 8 + d, 16 * q : 16 * q + 16, :] = tiles[d].astype(BF)

        def send(dz, dy):
            t = column + zs[dz] + ys[dy]
            remote(send_k.at[t], recv_k.at[slot], t, 1, k_recv.at[x * 2 + z]).start()

        for half in range(2):
            for dy in range(8):
                dz = (half + dy) % 2
                if dz or dy:
                    send(dz, dy)
                else:
                    pl.when(dx > 0)(functools.partial(send, dz, dy))
        return carry

    lax.fori_loop(0, 4, pack_spectrum, 0)
    own_k = pltpu.make_async_copy(send_k.at[me], recv_k.at[slot], own_sem.at[1])
    own_k.start()
    for load in loads[1:]:
        load.wait()

    def ring(step, way):
        src = max(0, 2 * step - 3 + way) if step > 1 else 0
        dst = min(7, 2 * step - 1 + way)
        here, there = w_ref.at[:, src], w_ref.at[:, dst]
        if step == 4:
            here, there = w_ref.at[way, src], w_ref.at[way, dst]
        to = wrap(y + (1 if way == 0 else 7), 8)
        return link(
            here, there, ring_send.at[way, step], ring_recv.at[way, step], x * 16 + z * 8 + to, ch
        )

    def ring_step(step):
        for way in range(2):
            if step > 1:
                ring(step - 1, way).wait_recv()
            ring(step, way).start()

    own_v.wait()
    all_here(recv_v, 0)
    own_w.wait()
    pair_w.wait_recv()
    time_ref[...] = recv_v[...].reshape(SEQ * 16, 128).astype(F32)

    def over_a(jj, carry):
        quad = jnp.concatenate(
            [time_ref[pl.ds(4 * jj + b, SEQ, stride=16), :].astype(BF) for b in range(4)], axis=1
        )
        both = jnp.concatenate([quad, quad], axis=0)
        got = jnp.dot(ahead_ref[...], both, preferred_element_type=F32)
        for b in range(4):
            re, im = got[:GRP, 128 * b : 128 * b + 128], got[GRP:, 128 * b : 128 * b + 128]
            tr, ti = twist_ref[4 * jj + b, 0], twist_ref[4 * jj + b, 1]
            rows = pl.ds(pl.multiple_of((4 * jj + b) * GRP, 8), GRP)
            first_ref[rows, 0:128] = re * tr - im * ti
            first_ref[rows, 128:256] = re * ti + im * tr
        return carry

    lax.fori_loop(0, 4, over_a, 0)

    def over_lanes(src, table, dst):
        def step(b, carry):
            rows = pl.ds(pl.multiple_of(b * 288, 16), 288)
            top, low = split(src[rows, :])
            dst[rows, :] = jnp.dot(
                jnp.concatenate([top, low], axis=1), table[...], preferred_element_type=F32
            )
            return carry

        lax.fori_loop(0, 4, step, 0)

    over_lanes(first_ref, lane_ahead_ref, second_ref)

    own_k.wait()
    base = GRP * 32
    filter_ref[pl.ds(64 * 32, 9 * 32), :] = jnp.zeros((9 * 32, 128), F32)
    filter_ref[pl.ds(base + 65 * 32, 7 * 32), :] = jnp.zeros((7 * 32, 128), F32)

    def row_here(buf, row, at, sems, own):
        def wait(count):
            part = buf.at[pl.ds(row * 8, count)]
            remote(part, part, me, at, sems.at[row]).wait_recv()

        if own:
            wait(7)
        else:
            wait(8)

    def row_of(dx, dz):
        return wrap(x + (4 - dx) % 4, 4) * 2 + z + dz - 2 * z * dz

    for dx in range(4):
        for dz in range(2):
            row = row_of(dx, dz)
            row_here(recv_k, row, 1, k_recv, dx + dz == 0)
            first_slot = jnp.where(row < 4, row * 8, 88 - row * 8)
            to = first_slot * 64 + jnp.where(row < 4, 0, base + 32 - 32 * 64)
            filter_ref[pl.ds(pl.multiple_of(to, 32), 512), :] = (
                recv_k[pl.ds(first_slot, 8)].reshape(512, 128).astype(F32)
            )
    ring_step(1)

    def filtered(b, carry):
        g = b * 8

        def rows(j):
            return pl.ds(pl.multiple_of(j * GRP + g, 8), 8)

        turned = []
        for j in range(16):
            re, im = second_ref[rows(j), 0:128], second_ref[rows(j), 128:256]
            if j:
                tr, ti = small_ref[0, j : j + 1, :], small_ref[1, j : j + 1, :]
                re, im = re * tr - im * ti, re * ti + im * tr
            turned.append((re, im))
        freq = fft(turned, -1)
        prod = []
        for h in range(16):
            re, im = freq[h]
            kr = (
                filter_ref[pl.ds(g * 32 + h, 8, stride=32), :]
                + filter_ref[pl.ds(base + g * 32 + 15 - h, 8, stride=32), :]
            )
            ki = (
                filter_ref[pl.ds(g * 32 + 16 + h, 8, stride=32), :]
                - filter_ref[pl.ds(base + g * 32 + 31 - h, 8, stride=32), :]
            )
            prod.append((re * kr - im * ki, re * ki + im * kr))
        spread = fft(prod, 1)
        for j in range(16):
            re, im = spread[j]
            if j:
                tr, ti = small_ref[0, j : j + 1, :], small_ref[1, j : j + 1, :]
                re, im = re * tr + im * ti, im * tr - re * ti
            first_ref[rows(j), 0:128] = re
            first_ref[rows(j), 128:256] = im
        return carry

    lax.fori_loop(0, GRP // 8, filtered, 0)
    over_lanes(first_ref, lane_back_ref, second_ref)

    def back_over_a(jj, carry):
        sides = []
        for b in range(4):
            rows = pl.ds(pl.multiple_of((4 * jj + b) * GRP, 8), GRP)
            re, im = second_ref[rows, 0:128], second_ref[rows, 128:256]
            tr, ti = twist_ref[4 * jj + b, 0], twist_ref[4 * jj + b, 1]
            sides.append(jnp.concatenate([re * tr + im * ti, im * tr - re * ti], axis=0))
        top, low = split(jnp.concatenate(sides, axis=1))
        got = jnp.dot(
            back_ref[...], jnp.concatenate([top, low, top], axis=0), preferred_element_type=F32
        )
        for b in range(4):
            time_ref[pl.ds(4 * jj + b, SEQ, stride=16), :] = got[:, 128 * b : 128 * b + 128]
        return carry

    lax.fori_loop(0, 4, back_over_a, 0)
    send_c[...] = time_ref[...].astype(BF).reshape(SEQ, 16, 128)
    own_c = pltpu.make_async_copy(send_c.at[me], recv_c.at[me], own_sem.at[2])
    own_c.start()
    each_partner(
        lambda t: remote(send_c.at[t], recv_c.at[me], t, 2, c_recv.at[x * 2 + z]).start()
    )
    ring_step(2)
    own_c.wait()

    for dx in range(4):
        for dz in range(2):
            row_here(recv_c, row_of(dx, dz), 2, c_recv, dx + dz == 0)

        for dz in range(2):
            lt = row_of(dx, dz)
            tiles = swap_lanes([recv_c[lt * 8 + d].astype(F32) for d in range(8)])
            scale = skip_ref[0:1, lanes(lt)]
            for i in range(8):
                rows = slice(16 * i, 16 * i + 16)
                held = values_ref[rows, lanes(lt)].astype(F32)
                mixed_ref[rows, lanes(lt)] = (
                    gate_ref[rows, lanes(lt)].astype(F32) * (tiles[i] + scale * held)
                ).astype(BF)

    def mixed_copy(d):
        if d % 2:
            src, dst = mixed_ref, recv_m.at[d]
        else:
            rows = pl.ds(0 if d == 2 else 64, 64)
            src, dst = recv_m.at[1 if d == 2 else 3, rows], recv_m.at[2, rows]
        to = wrap(x + (1 if d in (1, 2) else 3), 4)
        return link(src, dst, m_send.at[d], m_recv.at[d], to * 16 + low, ch)

    mixed_copy(1).start()
    mixed_copy(3).start()
    ring_step(3)

    spans = ((0, 5), (5, 8))

    def rows_of(part):
        return pl.ds(spans[part][0] * 64, (spans[part][1] - spans[part][0]) * 64)

    def half_copy(d, part):
        rows = rows_of(part)
        return link(
            half_send.at[d, rows], half_recv.at[d, rows], h_send.at[part, d], h_recv.at[part, d],
            me, zl * 2 + 1 - core,
        )

    def multiply(d, part):
        src = recv_m.at[d] if d else mixed_ref
        first, last = spans[part]
        rows = rows_of(part)
        for side in range(2):
            half = 1 - core if side == 0 else core
            got = lax.dot_general(
                w_ref[half, first:last].reshape((last - first) * 64, 1024), src[...],
                (((1,), (1,)), ((), ())), preferred_element_type=F32,
            )
            if side == 0:
                half_send[d, rows] = got.astype(BF)
                half_copy(d, part).start()
            else:
                own_half[d, rows] = got

    def z_copy(d, part, target):
        rows = rows_of(part)
        return link(
            z_send.at[d, rows], z_recv.at[zl, rows], zs_sem.at[part, d], zr_sem.at[part, zl],
            me, target * 2 + core,
        )

    def pass_on(d, part):
        half_copy(d, part).wait_recv()
        target = wrap(x + 4 - d, 4)
        rows = rows_of(part)
        total = own_half[d, rows] + half_recv[d, rows].astype(F32)

        @pl.when(target == zl)
        def _():
            done[rows, :] = total

        @pl.when(target != zl)
        def _():
            z_send[d, rows] = total.astype(BF)
            z_copy(d, part, target).start()

    multiply(0, 0)
    pass_on(0, 0)
    ring_step(4)
    mixed_copy(1).wait_recv()
    mixed_copy(2).start()
    mixed_copy(3).wait_recv()
    mixed_copy(0).start()
    multiply(1, 0)
    multiply(3, 0)
    pass_on(1, 0)
    pass_on(3, 0)
    for way in range(2):
        ring(4, way).wait_recv()
    multiply(0, 1)
    multiply(1, 1)
    multiply(3, 1)
    pass_on(0, 1)
    pass_on(1, 1)
    pass_on(3, 1)
    mixed_copy(2).wait_recv()
    mixed_copy(0).wait_recv()
    multiply(2, 0)
    multiply(2, 1)
    pass_on(2, 0)
    pass_on(2, 1)
    for part in range(2):
        rows = rows_of(part)
        for d in (1, 2, 3):
            peer = wrap(zl + d, 4)
            link(
                z_send.at[0, rows], z_recv.at[peer, rows], zs_sem.at[part, 0],
                zr_sem.at[part, peer], me, ch,
            ).wait_recv()
            done[rows, :] += z_recv[peer, rows].astype(F32)
    for slot_at, dy in enumerate((0, 7, 1, 6, 2, 5, 3, 4)):
        to = pl.multiple_of(wrap(y + dy, 8) * 64, 64)
        ordered[pl.ds(to, 64), :] = done[slot_at * 64 : slot_at * 64 + 64, :]

    @pl.when(cross)
    def _():
        final[...] = ordered[...].T.astype(BF)
        last = link(final, out_ref, o_sem.at[0], o_sem.at[1], zl * 16 + low, x * 2 + core)
        last.start()
        last.wait()

    @pl.when(jnp.logical_not(cross))
    def _():
        out_ref[...] = ordered[...].T.astype(BF)

    for d in range(4):
        mixed_copy(d).wait_send()
        for part in range(2):
            half_copy(d, part).wait_send()

            @pl.when(wrap(x + 4 - d, 4) != zl)
            def _(d=d, part=part):
                z_copy(d, part, zl).wait_send()

    all_sent(send_v, 0)
    all_sent(send_k, 1)
    all_sent(send_c, 2)
    pair_w.wait_send()
    for step in (1, 2, 3, 4):
        for way in range(2):
            ring(step, way).wait_send()


def block(values, gate, skip, spectrum, weight):
    consts = [jnp.asarray(t) for t in tables()]
    arrays = [values, gate, skip.reshape(1, -1), spectrum, weight] + consts
    vmem = lambda t: pltpu.VMEM(t.shape, t.dtype)
    held = [vmem(a) for a in arrays[:3]] + [pltpu.VMEM((8, 2, 2, 128, 128), F32)]
    held += [vmem(t) for t in consts]
    dma = pltpu.SemaphoreType.DMA
    return pl.pallas_call(
        block_kernel,
        out_shape=jax.ShapeDtypeStruct((128, 512), BF),
        in_specs=[pl.BlockSpec(memory_space=pltpu.HBM)] * len(arrays),
        out_specs=pl.BlockSpec(memory_space=pltpu.VMEM),
        scratch_shapes=held
        + [pltpu.VMEM((SEQ, 16, 128), BF)] * 2
        + [pltpu.VMEM((SEQ, 64, 128), BF)] * 2
        + [pltpu.VMEM((SEQ, 16, 128), BF)] * 2
        + [pltpu.VMEM((SEQ * 16, 128), F32)]
        + [pltpu.VMEM((2 * GRP * 32, 128), F32)]
        + [pltpu.VMEM((GRP * 16, 256), F32)] * 2
        + [
            pltpu.VMEM((2, 8, 64, 1024), BF),
            pltpu.VMEM((128, 1024), BF),
            pltpu.VMEM((4, 128, 1024), BF),
            pltpu.VMEM((4, 512, 128), BF),
            pltpu.VMEM((4, 512, 128), BF),
            pltpu.VMEM((4, 512, 128), F32),
            pltpu.VMEM((4, 512, 128), BF),
            pltpu.VMEM((4, 512, 128), BF),
            pltpu.VMEM((512, 128), F32),
            pltpu.VMEM((512, 128), F32),
            pltpu.VMEM((128, 512), BF),
        ]
        + [dma((9,)), dma((8,)), dma((4,)), dma((3,)), dma((3,))]
        + [dma((2, 5))] * 2
        + [dma((4,))] * 2
        + [dma((2, 4))] * 4
        + [dma((2,)), dma((8,)), dma((8,))],
        compiler_params=pltpu.CompilerParams(
            collective_id=0, has_side_effects=True, vmem_limit_bytes=63 * 2**20
        ),
        name="hyena_block",
    )(*arrays)


def solution(mesh):
    placed = (
        P("seq", "chan"),
        P("seq", "chan"),
        P("chan"),
        P(None, "seq", None, "chan"),
        P("seq", "chan"),
    )
    return jax.shard_map(
        block, mesh=mesh, in_specs=placed, out_specs=P("seq", "chan"), check_vma=False
    )
```

```python
import functools
import math

import jax
import jax.numpy as jnp
import numpy as np
from jax import lax
from jax.experimental import pallas as pl
from jax.experimental.pallas import tpu as pltpu
from jax.sharding import PartitionSpec as P

MESH = pl.DeviceIdType.MESH
BF = jnp.bfloat16
F32 = jnp.float32
SEQ = 64
GRP = 72


def wrap(a, n):
    return jnp.where(a >= n, a - n, a)


def split(x):
    top = x.astype(BF)
    return top, (x - top.astype(F32)).astype(BF)


def tables():
    g = np.arange(GRP)
    live = (g <= 64).astype(np.float64)[:, None]
    a = np.arange(SEQ)
    turn = 2.0 * np.pi * ((g[:, None] * a[None, :]) % 128) / 128
    ahead = np.concatenate([np.cos(turn) * live, -np.sin(turn) * live])
    top = ahead.astype(BF)
    low = (ahead - top.astype(np.float64)).astype(BF)
    ahead = np.concatenate([top, low], axis=1)
    back = np.concatenate([np.cos(turn) * live, -np.sin(turn) * live]).T / 16384.0
    top = back.astype(BF)
    low = (back - top.astype(np.float64)).astype(BF)
    back = np.concatenate([top, top, low], axis=1)
    lane = np.arange(128)
    i_of = lane // 16
    r = 16 * i_of[None, None, :] + np.arange(16)[:, None, None]
    theta = 2.0 * np.pi * ((r * g[None, :, None]) % 16384) / 16384
    twist = np.stack([np.cos(theta), -np.sin(theta)], axis=1).astype(np.float32)
    same = (lane[:, None] % 16 == lane[None, :] % 16).astype(np.float64)
    turn = 2.0 * np.pi * ((i_of[:, None] * i_of[None, :]) % 8) / 8
    c, s = np.cos(turn) * same, np.sin(turn) * same
    lane_ahead = np.block([[c, -s], [s, c]])
    lane_back = np.block([[c, s], [-s, c]])
    lane_ahead = np.concatenate([lane_ahead, lane_ahead]).astype(BF)
    lane_back = np.concatenate([lane_back, lane_back]).astype(BF)
    turn = 2.0 * np.pi * (np.arange(16)[:, None] * i_of[None, :]) / 128
    small = np.stack([np.cos(turn), -np.sin(turn)]).astype(np.float32)
    return ahead, back, twist, lane_ahead, lane_back, small


def swap_lanes(x):
    x = list(x)
    block = lax.broadcasted_iota(jnp.int32, x[0].shape, 1) // 16
    for bit in (1, 2, 4):
        clear = (block // bit) % 2 == 0
        for p in range(8):
            if p & bit:
                continue
            q = p | bit
            u, v = x[p], x[q]
            x[p] = jnp.where(clear, u, pltpu.roll(v, 16 * bit, 1))
            x[q] = jnp.where(clear, pltpu.roll(u, 128 - 16 * bit, 1), v)
    return x


def fft(z, sign):
    n = len(z)
    if n == 1:
        return z
    even, odd = fft(z[0::2], sign), fft(z[1::2], sign)
    out = [None] * n
    for k in range(n // 2):
        re, im = odd[k]
        if k == 0:
            pass
        elif 4 * k == n:
            re, im = (-im, re) if sign > 0 else (im, -re)
        elif 8 * k == n or 8 * k == 3 * n:
            h = math.sqrt(0.5)
            c = h if 8 * k == n else -h
            if sign > 0:
                re, im = re * c - im * h, im * c + re * h
            else:
                re, im = re * c + im * h, im * c - re * h
        else:
            c = math.cos(2 * math.pi * k / n)
            s = sign * math.sin(2 * math.pi * k / n)
            re, im = re * c - im * s, re * s + im * c
        out[k] = (even[k][0] + re, even[k][1] + im)
        out[k + n // 2] = (even[k][0] - re, even[k][1] - im)
    return out


def block_kernel(
    values_hbm, gate_hbm, skip_hbm, spec_hbm, weight_hbm,
    ahead_hbm, back_hbm, twist_hbm, lane_ahead_hbm, lane_back_hbm, small_hbm,
    out_ref,
    values_ref, gate_ref, skip_ref, spec_ref,
    ahead_ref, back_ref, twist_ref, lane_ahead_ref, lane_back_ref, small_ref,
    send_v, recv_v, send_k, recv_k, send_c, recv_c,
    time_ref, filter_ref, first_ref, second_ref,
    w_ref, mixed_ref, recv_m, half_send, half_recv, own_half, z_send, z_recv, done, ordered, final,
    in_sem, spec_sem, own_sem, send_sem, recv_sem,
    ring_send, ring_recv, m_send, m_recv, h_send, h_recv, zs_sem, zr_sem, o_sem, c_recv, k_recv,
):
    me, ch = lax.axis_index("seq"), lax.axis_index("chan")
    x, z, y = me // 16, (me // 8) % 2, me % 8
    low = me % 16
    zl, core = ch // 2, ch % 2
    cross = x + zl > 0

    xs = [wrap(x + d, 4) * 16 for d in range(4)]
    zs = [z * 8, 8 - z * 8]
    ys = [wrap(y + d, 8) for d in range(8)]
    partners = [
        xs[dx] + zs[dz] + ys[dy]
        for dx in range(4) for half in range(2) for dy in range(8)
        for dz in ((half + dy) % 2,) if dx or dz or dy
    ]

    def each_partner(fn):
        for t in partners:
            fn(t)

    loads = []
    for at, (src, dst) in enumerate((
        (values_hbm, values_ref), (gate_hbm, gate_ref), (skip_hbm, skip_ref),
        (ahead_hbm, ahead_ref), (back_hbm, back_ref), (twist_hbm, twist_ref),
        (lane_ahead_hbm, lane_ahead_ref), (lane_back_hbm, lane_back_ref),
        (small_hbm, small_ref),
    )):
        load = pltpu.make_async_copy(src, dst, in_sem.at[at])
        load.start()
        loads.append(load)
    spec_loads = []
    for lt in range(8):
        load = pltpu.make_async_copy(
            spec_hbm.at[:, :, :, pl.ds(128 * lt, 128)], spec_ref.at[lt], spec_sem.at[lt]
        )
        load.start()
        spec_loads.append(load)

    bar = pltpu.get_barrier_semaphore()

    def greet(seq, chan):
        pl.semaphore_signal(
            bar, inc=1, device_id={"seq": seq, "chan": chan}, device_id_type=MESH
        )

    each_partner(lambda t: greet(t, ch))
    for d in (1, 2, 3):
        greet(me, wrap(zl + d, 4) * 2 + core)
    greet(me, zl * 2 + 1 - core)

    @pl.when(cross)
    def _():
        greet(zl * 16 + low, wrap(zl + 4 - x, 4) * 2 + core)

    def link(src, dst, ss, rs, seq, chan):
        return pltpu.make_async_remote_copy(
            src_ref=src, dst_ref=dst, send_sem=ss, recv_sem=rs,
            device_id={"seq": seq, "chan": chan}, device_id_type=MESH,
        )

    def lanes(lt):
        return pl.ds(pl.multiple_of(128 * lt, 128), 128)

    def remote(src, dst, t, at, here=None):
        return pltpu.make_async_remote_copy(
            src_ref=src, dst_ref=dst, send_sem=send_sem.at[at],
            recv_sem=recv_sem.at[at] if here is None else here,
            device_id={"seq": t}, device_id_type=MESH,
        )

    def all_sent(src, at):
        remote(src.at[pl.ds(0, SEQ - 1)], src.at[pl.ds(0, SEQ - 1)], me, at).wait_send()

    def all_here(dst, at):
        remote(dst.at[pl.ds(0, SEQ - 1)], dst.at[pl.ds(0, SEQ - 1)], me, at).wait_recv()

    loads[0].wait()

    def pack_values(pair, carry):
        for lt in (2 * pair, 2 * pair + 1):
            tiles = swap_lanes(
                [values_ref[16 * i : 16 * i + 16, lanes(lt)].astype(F32) for i in range(8)]
            )
            for d in range(8):
                send_v[lt * 8 + d] = tiles[d].astype(BF)
        return carry

    lax.fori_loop(0, 4, pack_values, 0)
    own_v = pltpu.make_async_copy(send_v.at[me], recv_v.at[me], own_sem.at[0])
    own_v.start()
    pl.semaphore_wait(bar, jnp.where(cross, SEQ + 4, SEQ + 3))
    own_w = pltpu.make_async_copy(weight_hbm, w_ref.at[z, 0], own_sem.at[3])
    own_w.start()
    pair_w = link(
        weight_hbm, w_ref.at[z, 0], ring_send.at[0, 0], ring_recv.at[0, 0],
        x * 16 + (1 - z) * 8 + y, ch,
    )
    pair_w.start()
    each_partner(lambda t: remote(send_v.at[t], recv_v.at[me], t, 0).start())

    upper = me >= SEQ // 2
    slot = jnp.where(upper, 95 - me, me)
    for load in spec_loads:
        load.wait()

    def pack_spectrum(dx, carry):
        column = wrap(x + dx, 4) * 16
        for dz in range(2):
            lt = wrap(x + dx, 4) * 2 + z + dz - 2 * z * dz
            for q in range(4):
                gl, part = q // 2, q % 2
                source = jnp.where(upper, 1 - gl, gl)
                tiles = swap_lanes([
                    spec_ref[lt, part, source, pl.ds(jnp.where(upper, 7 - h, h), 16, stride=8), :]
                    for h in range(8)
                ])
                for d in range(8):
                    send_k[lt * 8 + d, 16 * q : 16 * q + 16, :] = tiles[d].astype(BF)

        def send(dz, dy):
            t = column + zs[dz] + ys[dy]
            remote(send_k.at[t], recv_k.at[slot], t, 1, k_recv.at[x * 2 + z]).start()

        for half in range(2):
            for dy in range(8):
                dz = (half + dy) % 2
                if dz or dy:
                    send(dz, dy)
                else:
                    pl.when(dx > 0)(functools.partial(send, dz, dy))
        return carry

    lax.fori_loop(0, 4, pack_spectrum, 0)
    own_k = pltpu.make_async_copy(send_k.at[me], recv_k.at[slot], own_sem.at[1])
    own_k.start()
    for load in loads[1:]:
        load.wait()

    def ring(step, way):
        src = max(0, 2 * step - 3 + way) if step > 1 else 0
        dst = min(7, 2 * step - 1 + way)
        here, there = w_ref.at[:, src], w_ref.at[:, dst]
        if step == 4:
            here, there = w_ref.at[way, src], w_ref.at[way, dst]
        to = wrap(y + (1 if way == 0 else 7), 8)
        return link(
            here, there, ring_send.at[way, step], ring_recv.at[way, step], x * 16 + z * 8 + to, ch
        )

    def ring_step(step):
        for way in range(2):
            if step > 1:
                ring(step - 1, way).wait_recv()
            ring(step, way).start()

    own_v.wait()
    all_here(recv_v, 0)
    own_w.wait()
    pair_w.wait_recv()
    time_ref[...] = recv_v[...].reshape(SEQ * 16, 128).astype(F32)

    def over_a(jj, carry):
        quad = jnp.concatenate(
            [time_ref[pl.ds(4 * jj + b, SEQ, stride=16), :].astype(BF) for b in range(4)], axis=1
        )
        both = jnp.concatenate([quad, quad], axis=0)
        got = jnp.dot(ahead_ref[...], both, preferred_element_type=F32)
        for b in range(4):
            re, im = got[:GRP, 128 * b : 128 * b + 128], got[GRP:, 128 * b : 128 * b + 128]
            tr, ti = twist_ref[4 * jj + b, 0], twist_ref[4 * jj + b, 1]
            rows = pl.ds(pl.multiple_of((4 * jj + b) * GRP, 8), GRP)
            first_ref[rows, 0:128] = re * tr - im * ti
            first_ref[rows, 128:256] = re * ti + im * tr
        return carry

    lax.fori_loop(0, 4, over_a, 0)

    def over_lanes(src, table, dst):
        def step(b, carry):
            rows = pl.ds(pl.multiple_of(b * 288, 16), 288)
            top, low = split(src[rows, :])
            dst[rows, :] = jnp.dot(
                jnp.concatenate([top, low], axis=1), table[...], preferred_element_type=F32
            )
            return carry

        lax.fori_loop(0, 4, step, 0)

    over_lanes(first_ref, lane_ahead_ref, second_ref)

    own_k.wait()
    base = GRP * 32
    filter_ref[pl.ds(64 * 32, 9 * 32), :] = jnp.zeros((9 * 32, 128), F32)
    filter_ref[pl.ds(base + 65 * 32, 7 * 32), :] = jnp.zeros((7 * 32, 128), F32)

    def row_here(buf, row, at, sems, own):
        def wait(count):
            part = buf.at[pl.ds(row * 8, count)]
            remote(part, part, me, at, sems.at[row]).wait_recv()

        if own:
            wait(7)
        else:
            wait(8)

    def row_of(dx, dz):
        return wrap(x + (4 - dx) % 4, 4) * 2 + z + dz - 2 * z * dz

    for dx in range(4):
        for dz in range(2):
            row = row_of(dx, dz)
            row_here(recv_k, row, 1, k_recv, dx + dz == 0)
            first_slot = jnp.where(row < 4, row * 8, 88 - row * 8)
            to = first_slot * 64 + jnp.where(row < 4, 0, base + 32 - 32 * 64)
            filter_ref[pl.ds(pl.multiple_of(to, 32), 512), :] = (
                recv_k[pl.ds(first_slot, 8)].reshape(512, 128).astype(F32)
            )
    ring_step(1)

    def filtered(b, carry):
        g = b * 8

        def rows(j):
            return pl.ds(pl.multiple_of(j * GRP + g, 8), 8)

        turned = []
        for j in range(16):
            re, im = second_ref[rows(j), 0:128], second_ref[rows(j), 128:256]
            if j:
                tr, ti = small_ref[0, j : j + 1, :], small_ref[1, j : j + 1, :]
                re, im = re * tr - im * ti, re * ti + im * tr
            turned.append((re, im))
        freq = fft(turned, -1)
        prod = []
        for h in range(16):
            re, im = freq[h]
            kr = (
                filter_ref[pl.ds(g * 32 + h, 8, stride=32), :]
                + filter_ref[pl.ds(base + g * 32 + 15 - h, 8, stride=32), :]
            )
            ki = (
                filter_ref[pl.ds(g * 32 + 16 + h, 8, stride=32), :]
                - filter_ref[pl.ds(base + g * 32 + 31 - h, 8, stride=32), :]
            )
            prod.append((re * kr - im * ki, re * ki + im * kr))
        spread = fft(prod, 1)
        for j in range(16):
            re, im = spread[j]
            if j:
                tr, ti = small_ref[0, j : j + 1, :], small_ref[1, j : j + 1, :]
                re, im = re * tr + im * ti, im * tr - re * ti
            first_ref[rows(j), 0:128] = re
            first_ref[rows(j), 128:256] = im
        return carry

    lax.fori_loop(0, GRP // 8, filtered, 0)
    over_lanes(first_ref, lane_back_ref, second_ref)

    def back_over_a(jj, carry):
        sides = []
        for b in range(4):
            rows = pl.ds(pl.multiple_of((4 * jj + b) * GRP, 8), GRP)
            re, im = second_ref[rows, 0:128], second_ref[rows, 128:256]
            tr, ti = twist_ref[4 * jj + b, 0], twist_ref[4 * jj + b, 1]
            sides.append(jnp.concatenate([re * tr + im * ti, im * tr - re * ti], axis=0))
        top, low = split(jnp.concatenate(sides, axis=1))
        got = jnp.dot(
            back_ref[...], jnp.concatenate([top, low, top], axis=0), preferred_element_type=F32
        )
        for b in range(4):
            time_ref[pl.ds(4 * jj + b, SEQ, stride=16), :] = got[:, 128 * b : 128 * b + 128]
        return carry

    lax.fori_loop(0, 4, back_over_a, 0)
    send_c[...] = time_ref[...].astype(BF).reshape(SEQ, 16, 128)
    own_c = pltpu.make_async_copy(send_c.at[me], recv_c.at[me], own_sem.at[2])
    own_c.start()
    each_partner(
        lambda t: remote(send_c.at[t], recv_c.at[me], t, 2, c_recv.at[x * 2 + z]).start()
    )
    ring_step(2)
    own_c.wait()

    def mixed_copy(d, columns=None):
        if d % 2:
            src, dst = mixed_ref, recv_m.at[d]
            if columns is not None:
                src, dst = src.at[:, columns], dst.at[:, columns]
        else:
            rows = pl.ds(0 if d == 2 else 64, 64)
            src, dst = recv_m.at[1 if d == 2 else 3, rows], recv_m.at[2, rows]
        to = wrap(x + (1 if d in (1, 2) else 3), 4)
        return link(src, dst, m_send.at[d], m_recv.at[d], to * 16 + low, ch)

    for dx in range(4):
        for dz in range(2):
            row_here(recv_c, row_of(dx, dz), 2, c_recv, dx + dz == 0)

        for dz in range(2):
            lt = row_of(dx, dz)
            tiles = swap_lanes([recv_c[lt * 8 + d].astype(F32) for d in range(8)])
            scale = skip_ref[0:1, lanes(lt)]
            for i in range(8):
                rows = slice(16 * i, 16 * i + 16)
                held = values_ref[rows, lanes(lt)].astype(F32)
                mixed_ref[rows, lanes(lt)] = (
                    gate_ref[rows, lanes(lt)].astype(F32) * (tiles[i] + scale * held)
                ).astype(BF)
        columns = pl.ds(pl.multiple_of(wrap(x + (4 - dx) % 4, 4) * 256, 256), 256)
        mixed_copy(1, columns).start()
        mixed_copy(3, columns).start()
        if dx == 2:
            ring_step(3)


    spans = ((0, 5), (5, 8))

    def rows_of(part):
        return pl.ds(spans[part][0] * 64, (spans[part][1] - spans[part][0]) * 64)

    def half_copy(d, part):
        rows = rows_of(part)
        return link(
            half_send.at[d, rows], half_recv.at[d, rows], h_send.at[part, d], h_recv.at[part, d],
            me, zl * 2 + 1 - core,
        )

    def multiply(d, part):
        src = recv_m.at[d] if d else mixed_ref
        first, last = spans[part]
        rows = rows_of(part)
        for side in range(2):
            half = 1 - core if side == 0 else core
            got = lax.dot_general(
                w_ref[half, first:last].reshape((last - first) * 64, 1024), src[...],
                (((1,), (1,)), ((), ())), preferred_element_type=F32,
            )
            if side == 0:
                half_send[d, rows] = got.astype(BF)
                half_copy(d, part).start()
            else:
                own_half[d, rows] = got

    def z_copy(d, part):
        rows = rows_of(part)
        return link(
            z_send.at[d, rows], z_recv.at[zl, rows], zs_sem.at[part, d], zr_sem.at[part, zl],
            me, 2 * d + core,
        )

    def pass_on(d, part):
        half_copy(d, part).wait_recv()
        rows = rows_of(part)
        total = own_half[d, rows] + half_recv[d, rows].astype(F32)

        @pl.when(zl == d)
        def _():
            done[rows, :] = total

        @pl.when(zl != d)
        def _():
            z_send[d, rows] = total.astype(BF)
            z_copy(d, part).start()

    multiply(0, 0)
    pass_on(0, 0)
    ring_step(4)
    mixed_copy(1).wait_recv()
    mixed_copy(2).start()
    mixed_copy(3).wait_recv()
    mixed_copy(0).start()
    multiply(1, 0)
    multiply(3, 0)
    pass_on(1, 0)
    pass_on(3, 0)
    for way in range(2):
        ring(4, way).wait_recv()
    multiply(0, 1)
    multiply(1, 1)
    multiply(3, 1)
    pass_on(0, 1)
    pass_on(1, 1)
    pass_on(3, 1)
    mixed_copy(2).wait_recv()
    mixed_copy(0).wait_recv()
    multiply(2, 0)
    multiply(2, 1)
    pass_on(2, 0)
    pass_on(2, 1)
    for part in range(2):
        rows = rows_of(part)
        for d in (1, 2, 3):
            peer = wrap(zl + d, 4)
            link(
                z_send.at[0, rows], z_recv.at[peer, rows], zs_sem.at[part, 0],
                zr_sem.at[part, peer], me, ch,
            ).wait_recv()
            done[rows, :] += z_recv[peer, rows].astype(F32)
    for slot_at, dy in enumerate((0, 7, 1, 6, 2, 5, 3, 4)):
        to = pl.multiple_of(wrap(y + dy, 8) * 64, 64)
        ordered[pl.ds(to, 64), :] = done[slot_at * 64 : slot_at * 64 + 64, :]

    @pl.when(cross)
    def _():
        final[...] = ordered[...].T.astype(BF)
        to = wrap(x + 4 - zl, 4) * 16 + low
        last = link(final, out_ref, o_sem.at[0], o_sem.at[1], to, x * 2 + core)
        last.start()
        last.wait()

    @pl.when(jnp.logical_not(cross))
    def _():
        out_ref[...] = ordered[...].T.astype(BF)

    for d in range(4):
        mixed_copy(d).wait_send()
        for part in range(2):
            half_copy(d, part).wait_send()

            @pl.when(zl != d)
            def _(d=d, part=part):
                z_copy(d, part).wait_send()

    all_sent(send_v, 0)
    all_sent(send_k, 1)
    all_sent(send_c, 2)
    pair_w.wait_send()
    for step in (1, 2, 3, 4):
        for way in range(2):
            ring(step, way).wait_send()


def block(values, gate, skip, spectrum, weight):
    consts = [jnp.asarray(t) for t in tables()]
    arrays = [values, gate, skip.reshape(1, -1), spectrum, weight] + consts
    vmem = lambda t: pltpu.VMEM(t.shape, t.dtype)
    held = [vmem(a) for a in arrays[:3]] + [pltpu.VMEM((8, 2, 2, 128, 128), F32)]
    held += [vmem(t) for t in consts]
    dma = pltpu.SemaphoreType.DMA
    return pl.pallas_call(
        block_kernel,
        out_shape=jax.ShapeDtypeStruct((128, 512), BF),
        in_specs=[pl.BlockSpec(memory_space=pltpu.HBM)] * len(arrays),
        out_specs=pl.BlockSpec(memory_space=pltpu.VMEM),
        scratch_shapes=held
        + [pltpu.VMEM((SEQ, 16, 128), BF)] * 2
        + [pltpu.VMEM((SEQ, 64, 128), BF)] * 2
        + [pltpu.VMEM((SEQ, 16, 128), BF)] * 2
        + [pltpu.VMEM((SEQ * 16, 128), F32)]
        + [pltpu.VMEM((2 * GRP * 32, 128), F32)]
        + [pltpu.VMEM((GRP * 16, 256), F32)] * 2
        + [
            pltpu.VMEM((2, 8, 64, 1024), BF),
            pltpu.VMEM((128, 1024), BF),
            pltpu.VMEM((4, 128, 1024), BF),
            pltpu.VMEM((4, 512, 128), BF),
            pltpu.VMEM((4, 512, 128), BF),
            pltpu.VMEM((4, 512, 128), F32),
            pltpu.VMEM((4, 512, 128), BF),
            pltpu.VMEM((4, 512, 128), BF),
            pltpu.VMEM((512, 128), F32),
            pltpu.VMEM((512, 128), F32),
            pltpu.VMEM((128, 512), BF),
        ]
        + [dma((9,)), dma((8,)), dma((4,)), dma((3,)), dma((3,))]
        + [dma((2, 5))] * 2
        + [dma((4,))] * 2
        + [dma((2, 4))] * 4
        + [dma((2,)), dma((8,)), dma((8,))],
        compiler_params=pltpu.CompilerParams(
            collective_id=0, has_side_effects=True, vmem_limit_bytes=63 * 2**20
        ),
        name="hyena_block",
    )(*arrays)


def solution(mesh):
    placed = (
        P("seq", "chan"),
        P("seq", "chan"),
        P("chan"),
        P(None, "seq", None, "chan"),
        P("seq", "chan"),
    )
    return jax.shard_map(
        block, mesh=mesh, in_specs=placed, out_specs=P("seq", "chan"), check_vma=False
    )
```

```python
import functools
import math

import jax
import jax.numpy as jnp
import numpy as np
from jax import lax
from jax.experimental import pallas as pl
from jax.experimental.pallas import tpu as pltpu
from jax.sharding import PartitionSpec as P

MESH = pl.DeviceIdType.MESH
BF = jnp.bfloat16
F32 = jnp.float32
SEQ = 64
GRP = 72


def wrap(a, n):
    return jnp.where(a >= n, a - n, a)


def split(x):
    top = x.astype(BF)
    return top, (x - top.astype(F32)).astype(BF)


def tables():
    g = np.arange(GRP)
    live = (g <= 64).astype(np.float64)[:, None]
    a = np.arange(SEQ)
    turn = 2.0 * np.pi * ((g[:, None] * a[None, :]) % 128) / 128
    ahead = np.concatenate([np.cos(turn) * live, -np.sin(turn) * live])
    top = ahead.astype(BF)
    low = (ahead - top.astype(np.float64)).astype(BF)
    ahead = np.concatenate([top, low], axis=1)
    back = np.concatenate([np.cos(turn) * live, -np.sin(turn) * live]).T / 16384.0
    top = back.astype(BF)
    low = (back - top.astype(np.float64)).astype(BF)
    back = np.concatenate([top, top, low], axis=1)
    lane = np.arange(128)
    i_of = lane // 16
    r = 16 * i_of[None, None, :] + np.arange(16)[:, None, None]
    theta = 2.0 * np.pi * ((r * g[None, :, None]) % 16384) / 16384
    twist = np.stack([np.cos(theta), -np.sin(theta)], axis=1).astype(np.float32)
    same = (lane[:, None] % 16 == lane[None, :] % 16).astype(np.float64)
    turn = 2.0 * np.pi * ((i_of[:, None] * i_of[None, :]) % 8) / 8
    c, s = np.cos(turn) * same, np.sin(turn) * same
    lane_ahead = np.block([[c, -s], [s, c]])
    lane_back = np.block([[c, s], [-s, c]])
    lane_ahead = np.concatenate([lane_ahead, lane_ahead]).astype(BF)
    lane_back = np.concatenate([lane_back, lane_back]).astype(BF)
    turn = 2.0 * np.pi * (np.arange(16)[:, None] * i_of[None, :]) / 128
    small = np.stack([np.cos(turn), -np.sin(turn)]).astype(np.float32)
    return ahead, back, twist, lane_ahead, lane_back, small


def swap_lanes(x):
    x = list(x)
    block = lax.broadcasted_iota(jnp.int32, x[0].shape, 1) // 16
    for bit in (1, 2, 4):
        clear = (block // bit) % 2 == 0
        for p in range(8):
            if p & bit:
                continue
            q = p | bit
            u, v = x[p], x[q]
            x[p] = jnp.where(clear, u, pltpu.roll(v, 16 * bit, 1))
            x[q] = jnp.where(clear, pltpu.roll(u, 128 - 16 * bit, 1), v)
    return x


def fft(z, sign):
    n = len(z)
    if n == 1:
        return z
    even, odd = fft(z[0::2], sign), fft(z[1::2], sign)
    out = [None] * n
    for k in range(n // 2):
        re, im = odd[k]
        if k == 0:
            pass
        elif 4 * k == n:
            re, im = (-im, re) if sign > 0 else (im, -re)
        elif 8 * k == n or 8 * k == 3 * n:
            h = math.sqrt(0.5)
            c = h if 8 * k == n else -h
            if sign > 0:
                re, im = re * c - im * h, im * c + re * h
            else:
                re, im = re * c + im * h, im * c - re * h
        else:
            c = math.cos(2 * math.pi * k / n)
            s = sign * math.sin(2 * math.pi * k / n)
            re, im = re * c - im * s, re * s + im * c
        out[k] = (even[k][0] + re, even[k][1] + im)
        out[k + n // 2] = (even[k][0] - re, even[k][1] - im)
    return out


def block_kernel(
    values_hbm, gate_hbm, skip_hbm, spec_hbm, weight_hbm,
    ahead_hbm, back_hbm, twist_hbm, lane_ahead_hbm, lane_back_hbm, small_hbm,
    out_ref,
    values_ref, gate_ref, skip_ref, spec_ref,
    ahead_ref, back_ref, twist_ref, lane_ahead_ref, lane_back_ref, small_ref,
    send_v, recv_v, send_k, recv_k, send_c, recv_c,
    time_ref, filter_ref, first_ref, second_ref,
    w_ref, mixed_ref, recv_m, half_send, half_recv, own_half, z_send, z_recv, done, ordered, final,
    in_sem, spec_sem, own_sem, send_sem, recv_sem,
    ring_send, ring_recv, m_send, m_recv, h_send, h_recv, zs_sem, zr_sem, o_sem, c_recv, k_recv,
):
    me, ch = lax.axis_index("seq"), lax.axis_index("chan")
    x, z, y = me // 16, (me // 8) % 2, me % 8
    low = me % 16
    zl, core = ch // 2, ch % 2
    cross = x + zl > 0

    xs = [wrap(x + d, 4) * 16 for d in range(4)]
    zs = [z * 8, 8 - z * 8]
    ys = [wrap(y + d, 8) for d in range(8)]
    partners = [
        xs[dx] + zs[dz] + ys[dy]
        for dx in range(4) for half in range(2) for dy in range(8)
        for dz in ((half + dy) % 2,) if dx or dz or dy
    ]

    def each_partner(fn):
        for t in partners:
            fn(t)

    loads = []
    for at, (src, dst) in enumerate((
        (values_hbm, values_ref), (gate_hbm, gate_ref), (skip_hbm, skip_ref),
        (ahead_hbm, ahead_ref), (back_hbm, back_ref), (twist_hbm, twist_ref),
        (lane_ahead_hbm, lane_ahead_ref), (lane_back_hbm, lane_back_ref),
        (small_hbm, small_ref),
    )):
        load = pltpu.make_async_copy(src, dst, in_sem.at[at])
        load.start()
        loads.append(load)
    spec_loads = []
    for lt in range(8):
        load = pltpu.make_async_copy(
            spec_hbm.at[:, :, :, pl.ds(128 * lt, 128)], spec_ref.at[lt], spec_sem.at[lt]
        )
        load.start()
        spec_loads.append(load)

    bar = pltpu.get_barrier_semaphore()

    def greet(seq, chan):
        pl.semaphore_signal(
            bar, inc=1, device_id={"seq": seq, "chan": chan}, device_id_type=MESH
        )

    each_partner(lambda t: greet(t, ch))
    for d in (1, 2, 3):
        greet(me, wrap(zl + d, 4) * 2 + core)
    greet(me, zl * 2 + 1 - core)

    @pl.when(cross)
    def _():
        greet(zl * 16 + low, wrap(zl + 4 - x, 4) * 2 + core)

    def link(src, dst, ss, rs, seq, chan):
        return pltpu.make_async_remote_copy(
            src_ref=src, dst_ref=dst, send_sem=ss, recv_sem=rs,
            device_id={"seq": seq, "chan": chan}, device_id_type=MESH,
        )

    def lanes(lt):
        return pl.ds(pl.multiple_of(128 * lt, 128), 128)

    def remote(src, dst, t, at, here=None):
        return pltpu.make_async_remote_copy(
            src_ref=src, dst_ref=dst, send_sem=send_sem.at[at],
            recv_sem=recv_sem.at[at] if here is None else here,
            device_id={"seq": t}, device_id_type=MESH,
        )

    def all_sent(src, at):
        remote(src.at[pl.ds(0, SEQ - 1)], src.at[pl.ds(0, SEQ - 1)], me, at).wait_send()

    def all_here(dst, at):
        remote(dst.at[pl.ds(0, SEQ - 1)], dst.at[pl.ds(0, SEQ - 1)], me, at).wait_recv()

    loads[0].wait()

    def pack_values(pair, carry):
        for lt in (2 * pair, 2 * pair + 1):
            tiles = swap_lanes(
                [values_ref[16 * i : 16 * i + 16, lanes(lt)].astype(F32) for i in range(8)]
            )
            for d in range(8):
                send_v[lt * 8 + d] = tiles[d].astype(BF)
        return carry

    lax.fori_loop(0, 4, pack_values, 0)
    own_v = pltpu.make_async_copy(send_v.at[me], recv_v.at[me], own_sem.at[0])
    own_v.start()
    pl.semaphore_wait(bar, jnp.where(cross, SEQ + 4, SEQ + 3))
    own_w = pltpu.make_async_copy(weight_hbm, w_ref.at[z, 0], own_sem.at[3])
    own_w.start()
    pair_w = link(
        weight_hbm, w_ref.at[z, 0], ring_send.at[0, 0], ring_recv.at[0, 0],
        x * 16 + (1 - z) * 8 + y, ch,
    )
    pair_w.start()
    each_partner(lambda t: remote(send_v.at[t], recv_v.at[me], t, 0).start())

    upper = me >= SEQ // 2
    slot = jnp.where(upper, 95 - me, me)
    for load in spec_loads:
        load.wait()

    def pack_spectrum(dx, carry):
        column = wrap(x + dx, 4) * 16
        for dz in range(2):
            lt = wrap(x + dx, 4) * 2 + z + dz - 2 * z * dz
            for q in range(4):
                gl, part = q // 2, q % 2
                source = jnp.where(upper, 1 - gl, gl)
                tiles = swap_lanes([
                    spec_ref[lt, part, source, pl.ds(jnp.where(upper, 7 - h, h), 16, stride=8), :]
                    for h in range(8)
                ])
                for d in range(8):
                    send_k[lt * 8 + d, 16 * q : 16 * q + 16, :] = tiles[d].astype(BF)

        def send(dz, dy):
            t = column + zs[dz] + ys[dy]
            remote(send_k.at[t], recv_k.at[slot], t, 1, k_recv.at[x * 2 + z]).start()

        for half in range(2):
            for dy in range(8):
                dz = (half + dy) % 2
                if dz or dy:
                    send(dz, dy)
                else:
                    pl.when(dx > 0)(functools.partial(send, dz, dy))
        return carry

    lax.fori_loop(0, 4, pack_spectrum, 0)
    own_k = pltpu.make_async_copy(send_k.at[me], recv_k.at[slot], own_sem.at[1])
    own_k.start()
    for load in loads[1:]:
        load.wait()

    def ring(step, way):
        src = max(0, 2 * step - 3 + way) if step > 1 else 0
        dst = min(7, 2 * step - 1 + way)
        here, there = w_ref.at[:, src], w_ref.at[:, dst]
        if step == 4:
            here, there = w_ref.at[way, src], w_ref.at[way, dst]
        to = wrap(y + (1 if way == 0 else 7), 8)
        return link(
            here, there, ring_send.at[way, step], ring_recv.at[way, step], x * 16 + z * 8 + to, ch
        )

    def ring_step(step):
        for way in range(2):
            if step > 1:
                ring(step - 1, way).wait_recv()
            ring(step, way).start()

    own_v.wait()
    all_here(recv_v, 0)
    own_w.wait()
    pair_w.wait_recv()
    time_ref[...] = recv_v[...].reshape(SEQ * 16, 128).astype(F32)

    def over_a(jj, carry):
        quad = jnp.concatenate(
            [time_ref[pl.ds(4 * jj + b, SEQ, stride=16), :].astype(BF) for b in range(4)], axis=1
        )
        both = jnp.concatenate([quad, quad], axis=0)
        got = jnp.dot(ahead_ref[...], both, preferred_element_type=F32)
        for b in range(4):
            re, im = got[:GRP, 128 * b : 128 * b + 128], got[GRP:, 128 * b : 128 * b + 128]
            tr, ti = twist_ref[4 * jj + b, 0], twist_ref[4 * jj + b, 1]
            rows = pl.ds(pl.multiple_of((4 * jj + b) * GRP, 8), GRP)
            first_ref[rows, 0:128] = re * tr - im * ti
            first_ref[rows, 128:256] = re * ti + im * tr
        return carry

    lax.fori_loop(0, 4, over_a, 0)

    def over_lanes(src, table, dst):
        def step(b, carry):
            rows = pl.ds(pl.multiple_of(b * 288, 16), 288)
            top, low = split(src[rows, :])
            dst[rows, :] = jnp.dot(
                jnp.concatenate([top, low], axis=1), table[...], preferred_element_type=F32
            )
            return carry

        lax.fori_loop(0, 4, step, 0)

    over_lanes(first_ref, lane_ahead_ref, second_ref)

    own_k.wait()
    base = GRP * 32
    filter_ref[pl.ds(64 * 32, 9 * 32), :] = jnp.zeros((9 * 32, 128), F32)
    filter_ref[pl.ds(base + 65 * 32, 7 * 32), :] = jnp.zeros((7 * 32, 128), F32)

    def row_here(buf, row, at, sems, own):
        def wait(count):
            part = buf.at[pl.ds(row * 8, count)]
            remote(part, part, me, at, sems.at[row]).wait_recv()

        if own:
            wait(7)
        else:
            wait(8)

    def row_of(dx, dz):
        return wrap(x + (4 - dx) % 4, 4) * 2 + z + dz - 2 * z * dz

    for dx in range(4):
        for dz in range(2):
            row = row_of(dx, dz)
            row_here(recv_k, row, 1, k_recv, dx + dz == 0)
            first_slot = jnp.where(row < 4, row * 8, 88 - row * 8)
            to = first_slot * 64 + jnp.where(row < 4, 0, base + 32 - 32 * 64)
            filter_ref[pl.ds(pl.multiple_of(to, 32), 512), :] = (
                recv_k[pl.ds(first_slot, 8)].reshape(512, 128).astype(F32)
            )
    ring_step(1)

    def filtered(b, carry):
        g = b * 8

        def rows(j):
            return pl.ds(pl.multiple_of(j * GRP + g, 8), 8)

        turned = []
        for j in range(16):
            re, im = second_ref[rows(j), 0:128], second_ref[rows(j), 128:256]
            if j:
                tr, ti = small_ref[0, j : j + 1, :], small_ref[1, j : j + 1, :]
                re, im = re * tr - im * ti, re * ti + im * tr
            turned.append((re, im))
        freq = fft(turned, -1)
        prod = []
        for h in range(16):
            re, im = freq[h]
            kr = (
                filter_ref[pl.ds(g * 32 + h, 8, stride=32), :]
                + filter_ref[pl.ds(base + g * 32 + 15 - h, 8, stride=32), :]
            )
            ki = (
                filter_ref[pl.ds(g * 32 + 16 + h, 8, stride=32), :]
                - filter_ref[pl.ds(base + g * 32 + 31 - h, 8, stride=32), :]
            )
            prod.append((re * kr - im * ki, re * ki + im * kr))
        spread = fft(prod, 1)
        for j in range(16):
            re, im = spread[j]
            if j:
                tr, ti = small_ref[0, j : j + 1, :], small_ref[1, j : j + 1, :]
                re, im = re * tr + im * ti, im * tr - re * ti
            first_ref[rows(j), 0:128] = re
            first_ref[rows(j), 128:256] = im
        return carry

    lax.fori_loop(0, GRP // 8, filtered, 0)
    over_lanes(first_ref, lane_back_ref, second_ref)

    def back_over_a(jj, carry):
        sides = []
        for b in range(4):
            rows = pl.ds(pl.multiple_of((4 * jj + b) * GRP, 8), GRP)
            re, im = second_ref[rows, 0:128], second_ref[rows, 128:256]
            tr, ti = twist_ref[4 * jj + b, 0], twist_ref[4 * jj + b, 1]
            sides.append(jnp.concatenate([re * tr + im * ti, im * tr - re * ti], axis=0))
        top, low = split(jnp.concatenate(sides, axis=1))
        got = jnp.dot(
            back_ref[...], jnp.concatenate([top, low, top], axis=0), preferred_element_type=F32
        )
        for b in range(4):
            time_ref[pl.ds(4 * jj + b, SEQ, stride=16), :] = got[:, 128 * b : 128 * b + 128]
        return carry

    lax.fori_loop(0, 4, back_over_a, 0)
    send_c[...] = time_ref[...].astype(BF).reshape(SEQ, 16, 128)
    own_c = pltpu.make_async_copy(send_c.at[me], recv_c.at[me], own_sem.at[2])
    own_c.start()
    each_partner(
        lambda t: remote(send_c.at[t], recv_c.at[me], t, 2, c_recv.at[x * 2 + z]).start()
    )
    ring_step(2)
    own_c.wait()

    def mixed_copy(d, columns=None):
        if d % 2:
            src, dst = mixed_ref, recv_m.at[d]
            if columns is not None:
                src, dst = src.at[:, columns], dst.at[:, columns]
        else:
            rows = pl.ds(0 if d == 2 else 64, 64)
            src, dst = recv_m.at[1 if d == 2 else 3, rows], recv_m.at[2, rows]
        to = wrap(x + (1 if d in (1, 2) else 3), 4)
        return link(src, dst, m_send.at[d], m_recv.at[d], to * 16 + low, ch)

    for dx in range(4):
        for dz in range(2):
            row_here(recv_c, row_of(dx, dz), 2, c_recv, dx + dz == 0)

        for dz in range(2):
            lt = row_of(dx, dz)
            tiles = swap_lanes([recv_c[lt * 8 + d].astype(F32) for d in range(8)])
            scale = skip_ref[0:1, lanes(lt)]
            for i in range(8):
                rows = slice(16 * i, 16 * i + 16)
                held = values_ref[rows, lanes(lt)].astype(F32)
                mixed_ref[rows, lanes(lt)] = (
                    gate_ref[rows, lanes(lt)].astype(F32) * (tiles[i] + scale * held)
                ).astype(BF)
        columns = pl.ds(pl.multiple_of(wrap(x + (4 - dx) % 4, 4) * 256, 256), 256)
        mixed_copy(1, columns).start()
        mixed_copy(3, columns).start()
        if dx == 2:
            ring_step(3)


    spans = ((0, 5), (5, 8))

    def rows_of(part):
        return pl.ds(spans[part][0] * 64, (spans[part][1] - spans[part][0]) * 64)

    def half_copy(d, part):
        rows = rows_of(part)
        return link(
            half_send.at[d, rows], half_recv.at[d, rows], h_send.at[part, d], h_recv.at[part, d],
            me, zl * 2 + 1 - core,
        )

    def multiply(d, part):
        src = recv_m.at[d] if d else mixed_ref
        first, last = spans[part]
        rows = rows_of(part)
        for side in range(2):
            half = 1 - core if side == 0 else core
            got = lax.dot_general(
                w_ref[half, first:last].reshape((last - first) * 64, 1024), src[...],
                (((1,), (1,)), ((), ())), preferred_element_type=F32,
            )
            if side == 0:
                half_send[d, rows] = got.astype(BF)
                half_copy(d, part).start()
            else:
                own_half[d, rows] = got

    def z_copy(d, part):
        rows = rows_of(part)
        return link(
            z_send.at[d, rows], z_recv.at[zl, rows], zs_sem.at[part, d], zr_sem.at[part, zl],
            me, 2 * d + core,
        )

    def pass_on(d, part):
        half_copy(d, part).wait_recv()
        rows = rows_of(part)
        total = own_half[d, rows] + half_recv[d, rows].astype(F32)

        @pl.when(zl == d)
        def _():
            done[rows, :] = total

        @pl.when(zl != d)
        def _():
            z_send[d, rows] = total.astype(BF)
            z_copy(d, part).start()

    multiply(0, 0)
    pass_on(0, 0)
    ring_step(4)
    mixed_copy(1).wait_recv()
    mixed_copy(2).start()
    mixed_copy(3).wait_recv()
    mixed_copy(0).start()
    multiply(1, 0)
    multiply(3, 0)
    pass_on(1, 0)
    pass_on(3, 0)
    for way in range(2):
        ring(4, way).wait_recv()
    multiply(0, 1)
    multiply(1, 1)
    multiply(3, 1)
    pass_on(0, 1)
    pass_on(1, 1)
    pass_on(3, 1)
    mixed_copy(2).wait_recv()
    mixed_copy(0).wait_recv()
    multiply(2, 0)
    multiply(2, 1)
    pass_on(2, 0)
    pass_on(2, 1)
    for part in range(2):
        rows = rows_of(part)
        for d in (1, 2, 3):
            peer = wrap(zl + d, 4)
            link(
                z_send.at[0, rows], z_recv.at[peer, rows], zs_sem.at[part, 0],
                zr_sem.at[part, peer], me, ch,
            ).wait_recv()
            done[rows, :] += z_recv[peer, rows].astype(F32)
    for slot_at, dy in enumerate((0, 7, 1, 6, 2, 5, 3, 4)):
        to = pl.multiple_of(wrap(y + dy, 8) * 64, 64)
        ordered[pl.ds(to, 64), :] = done[slot_at * 64 : slot_at * 64 + 64, :]

    @pl.when(cross)
    def _():
        final[...] = ordered[...].astype(BF)
        to = wrap(x + 4 - zl, 4) * 16 + low
        last = link(final, out_ref, o_sem.at[0], o_sem.at[1], to, x * 2 + core)
        last.start()
        last.wait()

    @pl.when(jnp.logical_not(cross))
    def _():
        out_ref[...] = ordered[...].astype(BF)

    for d in range(4):
        mixed_copy(d).wait_send()
        for part in range(2):
            half_copy(d, part).wait_send()

            @pl.when(zl != d)
            def _(d=d, part=part):
                z_copy(d, part).wait_send()

    all_sent(send_v, 0)
    all_sent(send_k, 1)
    all_sent(send_c, 2)
    pair_w.wait_send()
    for step in (1, 2, 3, 4):
        for way in range(2):
            ring(step, way).wait_send()


def block(values, gate, skip, spectrum, weight):
    consts = [jnp.asarray(t) for t in tables()]
    arrays = [values, gate, skip.reshape(1, -1), spectrum, weight] + consts
    vmem = lambda t: pltpu.VMEM(t.shape, t.dtype)
    held = [vmem(a) for a in arrays[:3]] + [pltpu.VMEM((8, 2, 2, 128, 128), F32)]
    held += [vmem(t) for t in consts]
    dma = pltpu.SemaphoreType.DMA
    return pl.pallas_call(
        block_kernel,
        out_shape=jax.ShapeDtypeStruct((512, 128), BF),
        in_specs=[pl.BlockSpec(memory_space=pltpu.HBM)] * len(arrays),
        out_specs=pl.BlockSpec(memory_space=pltpu.VMEM),
        scratch_shapes=held
        + [pltpu.VMEM((SEQ, 16, 128), BF)] * 2
        + [pltpu.VMEM((SEQ, 64, 128), BF)] * 2
        + [pltpu.VMEM((SEQ, 16, 128), BF)] * 2
        + [pltpu.VMEM((SEQ * 16, 128), F32)]
        + [pltpu.VMEM((2 * GRP * 32, 128), F32)]
        + [pltpu.VMEM((GRP * 16, 256), F32)] * 2
        + [
            pltpu.VMEM((2, 8, 64, 1024), BF),
            pltpu.VMEM((128, 1024), BF),
            pltpu.VMEM((4, 128, 1024), BF),
            pltpu.VMEM((4, 512, 128), BF),
            pltpu.VMEM((4, 512, 128), BF),
            pltpu.VMEM((4, 512, 128), F32),
            pltpu.VMEM((4, 512, 128), BF),
            pltpu.VMEM((4, 512, 128), BF),
            pltpu.VMEM((512, 128), F32),
            pltpu.VMEM((512, 128), F32),
            pltpu.VMEM((512, 128), BF),
        ]
        + [dma((9,)), dma((8,)), dma((4,)), dma((3,)), dma((3,))]
        + [dma((2, 5))] * 2
        + [dma((4,))] * 2
        + [dma((2, 4))] * 4
        + [dma((2,)), dma((8,)), dma((8,))],
        compiler_params=pltpu.CompilerParams(
            collective_id=0, has_side_effects=True, vmem_limit_bytes=63 * 2**20
        ),
        name="hyena_block",
    )(*arrays).T


def solution(mesh):
    placed = (
        P("seq", "chan"),
        P("seq", "chan"),
        P("chan"),
        P(None, "seq", None, "chan"),
        P("seq", "chan"),
    )
    return jax.shard_map(
        block, mesh=mesh, in_specs=placed, out_specs=P("seq", "chan"), check_vma=False
    )
```
